128 devices in a mesh: group: 8 (over x, y_hi), view: 2 (over core), patch: 8 (over z, y_lo).
Axes of the slice: x: 4, y: 4 (y_hi: 2, y_lo: 2; y = y_hi * 2 + y_lo), z: 4, core: 2. Of those that a mesh axis runs over, the one named last changes fastest.
Arguments:
- hidden: bfloat16 [32, 1024, 1024], P(('group', 'view'), 'patch'), parts along dimension 0, may hold values from -10.2 to 10.2
- rays: bfloat16 [32, 1024, 1024], P(('group', 'view'), 'patch'), parts along dimension 0, may hold values from -3 to 3
- view_set: int32 [32], P('group'), parts along dimension 0, may hold values from 0 to 1, as said below
- obs_keys: bfloat16 [3, 1024, 1024], P(None, 'patch'), may hold values from -10 to 10
- obs_values: bfloat16 [3, 1024, 1024], P(None, 'patch'), may hold values from -6 to 6
- w_query: bfloat16 [1024, 1024], replicated, may hold values from -0.25 to 0.25
- w_key: bfloat16 [1024, 1024], replicated, may hold values from -0.3125 to 0.3125
- w_value: bfloat16 [1024, 1024], replicated, may hold values from -0.1875 to 0.1875
- w_out: bfloat16 [1024, 1024], replicated, may hold values from -0.5 to 0.5
Outputs:
- attended: bfloat16 [32, 1024, 1024], P(('group', 'view'), 'patch'), parts along dimension 0
The draws below stay inside these ranges and needn't reach their ends.
There are 8 independent parts, one for each index of `group`. The reference program is written for one: setup_inputs(seed, part) draws one part's arguments, and reference() takes and returns one part's arrays. A program takes and returns all parts, laid end to end along the dimension named above; an argument that names none is the same for every part. Nothing has to cross between parts.
Inputs may be any that keep to these rules, and one draw needn't show every extreme that they name: `view_set`: every set has at least one view.
All inputs are finite; a program needn't handle non-finite values.
Results may differ from the reference program's by a relative error of at most 0.0075.
The reference program's roundings to bfloat16 on the way count: a program that leaves them out, or rounds other values in their place, can miss the bound.
Values may be sent and summed in bfloat16 or wider, within the bound.
No kernel may reach another device: no remote copies, remote signals or barrier semaphores. Data moves between devices by JAX's collectives and lax.ppermute only.
A program may use at most 320 MiB of HBM per device.

```python
import math
import jax
import jax.numpy as jnp
from jax import lax

D = 1024
HEADS = 16
HEAD_DIM = 64
OBS = 3
VIEWS = 4
TOK_VIEW = 1024


def draw_hidden(key, part):
    key = jax.random.fold_in(key, 11)
    first = jax.random.fold_in(key, 0)
    return jnp.clip(jax.random.normal(first, (VIEWS, TOK_VIEW, D), jnp.float32), -6.0, 6.0).astype(jnp.bfloat16)


def draw_view_set(key, part):
    key = jax.random.fold_in(key, 23)
    first, second = jax.random.split(key)
    labels = jax.random.randint(first, (VIEWS,), 0, 2, dtype=jnp.int32)
    order = jax.random.permutation(second, jnp.arange(VIEWS, dtype=jnp.int32))
    positions = jnp.arange(VIEWS, dtype=jnp.int32)
    labels = jnp.where(positions == order[0], 0, labels)
    labels = jnp.where(positions == order[1], 1, labels)
    return labels.astype(jnp.int32)


def block_levels(key, dims, cuts, smallest, largest):
    factor_of, own = 1.0, jax.random.fold_in(key, 6)
    for position, shards_of in cuts:
        steps = jnp.exp(jax.random.uniform(jax.random.fold_in(own, position), (shards_of,), jnp.float32, smallest / len(cuts), largest / len(cuts)))
        factor_of = factor_of * jnp.repeat(steps, dims[position] // shards_of).reshape([-1 if axis == position else 1 for axis in range(len(dims))])
    return factor_of


def gaussian(stream_key, shape, spread, reach, cuts=(), kind=jnp.bfloat16):
    array = spread * jax.random.normal(stream_key, shape, jnp.float32)
    if cuts:
        array = array * block_levels(stream_key, shape, cuts, -0.22, 0.18)
    return jnp.clip(array, -reach, reach).astype(kind)


def setup_inputs(seed: int = 0, part: int = 0) -> dict:
    key_of = jax.random.split(jax.random.key(seed), 10)
    part_keys = jax.random.split(jax.random.fold_in(key_of[9], part), 10)
    hidden = draw_hidden(jax.random.fold_in(jax.random.fold_in(key_of[9], part), 71), part)
    rays = gaussian(part_keys[1], (VIEWS, TOK_VIEW, D), 0.5, 3.0, ((0, 2), (1, 8)))
    view_set = draw_view_set(jax.random.fold_in(jax.random.fold_in(key_of[9], part), 71), part)
    obs_keys = gaussian(key_of[3], (OBS, TOK_VIEW, D), 1.7, 10.0, ((1, 8),))
    obs_values = gaussian(key_of[4], (OBS, TOK_VIEW, D), 1.0, 6.0, ((1, 8),))
    w_query = gaussian(key_of[5], (D, D), (D // 2) ** -0.5, 0.25)
    w_key = gaussian(key_of[6], (D, D), (D // 3) ** -0.5, 0.3125)
    w_value = gaussian(key_of[7], (D, D), D ** -0.5, 0.1875)
    w_out = gaussian(key_of[8], (D, D), (D // 8) ** -0.5, 0.5)
    return {"hidden": hidden, "rays": rays, "view_set": view_set, "obs_keys": obs_keys, "obs_values": obs_values, "w_query": w_query, "w_key": w_key, "w_value": w_value, "w_out": w_out}


def reference(hidden, rays, view_set, obs_keys, obs_values, w_query, w_key, w_value, w_out):
    source = (hidden.astype(jnp.float32) + rays.astype(jnp.float32)).astype(jnp.bfloat16)
    flat = source.reshape(VIEWS * TOK_VIEW, D)
    queries = jnp.dot(flat, w_query, preferred_element_type=jnp.float32).astype(jnp.bfloat16)
    keys = jnp.dot(flat, w_key, preferred_element_type=jnp.float32).astype(jnp.bfloat16)
    values = jnp.dot(flat, w_value, preferred_element_type=jnp.float32).astype(jnp.bfloat16)
    token_view = (jnp.arange(VIEWS * TOK_VIEW, dtype=jnp.int32) // TOK_VIEW).astype(jnp.int32)
    token_set = view_set[token_view]
    visible = token_set[:, None] == token_set[None, :]
    obs_k = obs_keys.reshape(OBS * TOK_VIEW, HEADS, HEAD_DIM).transpose(1, 0, 2)
    obs_v = obs_values.reshape(OBS * TOK_VIEW, HEADS, HEAD_DIM).transpose(1, 0, 2)
    q_heads = queries.reshape(-1, HEADS, HEAD_DIM).transpose(1, 0, 2)
    k_heads = keys.reshape(-1, HEADS, HEAD_DIM).transpose(1, 0, 2)
    v_heads = values.reshape(-1, HEADS, HEAD_DIM).transpose(1, 0, 2)
    factor = 1.0 / math.sqrt(HEAD_DIM)

    def one_head(view_entries):
        query_heads_local, key_heads_local, value_heads_local, observed_key_heads, observed_value_heads = view_entries
        scores = jnp.dot(query_heads_local, key_heads_local.T, preferred_element_type=jnp.float32) * factor
        scores = jnp.where(visible, scores, -1e+30)
        obs_scores = jnp.dot(query_heads_local, observed_key_heads.T, preferred_element_type=jnp.float32) * factor
        top = jnp.maximum(lax.optimization_barrier(jnp.max(scores, axis=1)), lax.optimization_barrier(jnp.max(obs_scores, axis=1)))
        weights = jnp.exp(scores - top[:, None])
        observed_probabilities = jnp.exp(obs_scores - top[:, None])
        total = lax.optimization_barrier(jnp.sum(weights, axis=1)) + lax.optimization_barrier(jnp.sum(observed_probabilities, axis=1))
        blended_output = jnp.dot(weights.astype(jnp.bfloat16), value_heads_local, preferred_element_type=jnp.float32)
        blended_output = blended_output + jnp.dot(observed_probabilities.astype(jnp.bfloat16), observed_value_heads, preferred_element_type=jnp.float32)
        return (blended_output / total[:, None]).astype(jnp.bfloat16)
    context = lax.map(one_head, (q_heads, k_heads, v_heads, obs_k, obs_v))
    context = context.transpose(1, 0, 2).reshape(VIEWS * TOK_VIEW, D)
    attended = jnp.dot(context, w_out, preferred_element_type=jnp.float32).astype(jnp.bfloat16)
    return attended.reshape(VIEWS, TOK_VIEW, D)
```

```python
import functools

import jax
import jax.numpy as jnp
from jax import lax
from jax.experimental import pallas as pl
from jax.experimental.pallas import tpu as pltpu
from jax.sharding import PartitionSpec as P

HEADS = 16
HEAD_DIM = 64
SUM_ROW = HEAD_DIM
VALUE_ROWS = HEAD_DIM + 16
KEY_COLS = 2 * HEAD_DIM
LIMIT = 2.0**100
BF16 = jnp.bfloat16
F32 = jnp.float32
MIB = 2**20


def dot(a, b):
    return jnp.dot(a, b, preferred_element_type=F32)


def params(mib):
    return pltpu.CompilerParams(vmem_limit_bytes=mib * MIB)


def cost(flops, nbytes):
    return pl.CostEstimate(flops=int(flops), bytes_accessed=int(nbytes), transcendentals=0)


def make_source(hidden, rays, source):
    both = hidden[...].astype(F32) + rays[...].astype(F32)
    source[...] = both.astype(BF16).reshape(source.shape)


def project_heads(source, weight, scale):
    rows = dot(source[...], weight[...]).astype(BF16)
    if scale != 1.0:
        rows = rows * jnp.asarray(scale, BF16)
    return rows.T


def pack_queries_kernel(view, hidden, rays, weight, obs_k, obs_v, out, source):
    step = pl.program_id(0)

    @pl.when(step == 0)
    def _():
        make_source(hidden, rays, source)

    tok = hidden.shape[1]
    feats = project_heads(source, weight, HEAD_DIM**-0.5)
    for head in range(out.shape[0]):
        rows = slice(head * HEAD_DIM, (head + 1) * HEAD_DIM)
        for i in range(hidden.shape[0]):
            out[head, i * HEAD_DIM : (i + 1) * HEAD_DIM, :] = feats[rows, i * tok : (i + 1) * tok]
    base = hidden.shape[0] * HEAD_DIM

    def observed(ref):
        for o in range(ref.shape[0]):
            turned = ref[o].T
            for head in range(out.shape[0]):
                out[head, base + o * HEAD_DIM : base + (o + 1) * HEAD_DIM, :] = turned[
                    head * HEAD_DIM : (head + 1) * HEAD_DIM
                ]

    @pl.when(view[0] == 0)
    def _():
        observed(obs_k)

    @pl.when(view[0] != 0)
    def _():
        observed(obs_v)


def pack_queries(view, hidden, rays, weight, obs_k, obs_v):
    views, tok, width = hidden.shape
    obs = obs_k.shape[0]
    steps = 4
    cols = width // steps
    heads = HEADS // steps
    rows = (views + obs) * HEAD_DIM
    whole = pl.BlockSpec((views, tok, width), lambda j, v: (0, 0, 0))
    return pl.pallas_call(
        pack_queries_kernel,
        grid_spec=pltpu.PrefetchScalarGridSpec(
            num_scalar_prefetch=1,
            grid=(steps,),
            in_specs=[
                whole,
                whole,
                pl.BlockSpec((width, cols), lambda j, v: (0, j)),
                pl.BlockSpec((obs, tok, cols), lambda j, v: (0, 0, j * (1 - v[0]))),
                pl.BlockSpec((obs, tok, cols), lambda j, v: (0, 0, j * v[0])),
            ],
            out_specs=pl.BlockSpec((heads, rows, tok), lambda j, v: (j, 0, 0)),
            scratch_shapes=[pltpu.VMEM((views * tok, width), BF16)],
        ),
        out_shape=jax.ShapeDtypeStruct((HEADS, rows, tok), BF16),
        compiler_params=params(24),
        cost_estimate=cost(2 * views * tok * width * width, 6 * MIB),
        name="pack_queries",
    )(view, hidden, rays, weight, obs_k, obs_v)


def pack_pairs_kernel(hidden, rays, w_key, w_value, out, source):
    @pl.when(pl.program_id(0) == 0)
    def _():
        make_source(hidden, rays, source)

    views, tok = hidden.shape[:2]
    for place, weight in enumerate((w_key, w_value)):
        feats = project_heads(source, weight, 1.0)
        for head in range(out.shape[0]):
            rows = slice(head * HEAD_DIM, (head + 1) * HEAD_DIM)
            for i in range(views):
                at = (place * views + i) * HEAD_DIM
                out[head, at : at + HEAD_DIM, :] = feats[rows, i * tok : (i + 1) * tok]


def pack_pairs(hidden, rays, w_key, w_value):
    views, tok, width = hidden.shape
    steps = 4
    cols = width // steps
    heads = HEADS // steps
    rows = 2 * views * HEAD_DIM
    whole = pl.BlockSpec((views, tok, width), lambda j: (0, 0, 0))
    column = pl.BlockSpec((width, cols), lambda j: (0, j))
    return pl.pallas_call(
        pack_pairs_kernel,
        grid=(steps,),
        in_specs=[whole, whole, column, column],
        out_specs=pl.BlockSpec((heads, rows, tok), lambda j: (j, 0, 0)),
        scratch_shapes=[pltpu.VMEM((views * tok, width), BF16)],
        out_shape=jax.ShapeDtypeStruct((HEADS, rows, tok), BF16),
        compiler_params=params(24),
        cost_estimate=cost(4 * views * tok * width * width, 7 * MIB),
        name="pack_pairs",
    )(hidden, rays, w_key, w_value)


def ones_rows(count, ones, lanes):
    row = lax.broadcasted_iota(jnp.int32, (count, lanes), 0)
    return jnp.where(row < ones, 1.0, 0.0).astype(BF16)


def store_keys(keys, at, turned):
    tok = turned.shape[1]
    full = jnp.concatenate([turned, ones_rows(KEY_COLS - HEAD_DIM, 3, tok)], axis=0)
    keys[at : at + tok, :] = full.T


def offset_rows(top):
    first = top.astype(BF16)
    rest = top - first.astype(F32)
    second = rest.astype(BF16)
    third = rest - second.astype(F32)
    row = lax.broadcasted_iota(jnp.int32, (KEY_COLS - HEAD_DIM, top.shape[1]), 0)
    picked = jnp.where(row == 0, first.astype(F32), 0.0)
    picked = jnp.where(row == 1, second.astype(F32), picked)
    picked = jnp.where(row == 2, third, picked)
    return (-picked).astype(BF16)


def block_max(keys, at, count, block, query, top):
    def step(i, top):
        start = pl.multiple_of(at + i * block, block)
        scores = dot(keys[pl.ds(start, block), :], query)
        return jnp.maximum(top, jnp.max(scores, axis=0, keepdims=True))

    return lax.fori_loop(0, count // block, step, top)


def weighted(keys, values, start, count, query):
    weights = jnp.exp(dot(keys[pl.ds(start, count), :], query)).astype(BF16)
    return dot(values[:, pl.ds(start, count)], weights)


def observed_kernel(packed, query_out, sums, keys, values):
    patches = packed.shape[0] // 2
    tok = packed.shape[2]
    views = query_out.shape[0]
    here = views // 2
    obs = packed.shape[1] // HEAD_DIM - here
    span = patches * tok
    for o in range(obs):
        rows = slice((here + o) * HEAD_DIM, (here + o + 1) * HEAD_DIM)
        for p in range(patches):
            at = (o * patches + p) * tok
            store_keys(keys, at, packed[p, rows, :])
            values[0:HEAD_DIM, at : at + tok] = packed[patches + p, rows, :]
    values[HEAD_DIM:, :] = jnp.ones((VALUE_ROWS - HEAD_DIM, obs * span), BF16)
    for u in range(views):
        rows = slice((u % here) * HEAD_DIM, (u % here + 1) * HEAD_DIM)
        query = jnp.concatenate([packed[(u // here) * patches + p, rows, :] for p in range(patches)], axis=1)
        query_out[u, 0:HEAD_DIM, :] = query
        top = jnp.max(dot(keys[0:tok, 0:HEAD_DIM], query), axis=0, keepdims=True)
        query_out[u, HEAD_DIM:, :] = offset_rows(top)

    def one_view(u, block):
        query = query_out[u]
        total = None
        for o in range(obs * span // block):
            term = weighted(keys, values, o * block, block, query)
            total = term if total is None else total + term
        sums[u] = total

    @pl.loop(0, views)
    def _(u):
        one_view(u, span)

    largest = jnp.max(sums[:, SUM_ROW : SUM_ROW + 1, :])

    @pl.when(jnp.logical_not(largest < LIMIT))
    def _():
        @pl.loop(0, views)
        def _(u):
            query_out[u, HEAD_DIM:, :] = jnp.zeros((KEY_COLS - HEAD_DIM, span), BF16)
            low = jnp.full((1, span), -jnp.inf, F32)
            top = block_max(keys, 0, obs * span, tok, query_out[u], low)
            query_out[u, HEAD_DIM:, :] = offset_rows(top)
            sums[u] = jnp.zeros(sums.shape[1:], F32)

            @pl.loop(0, obs * patches)
            def _(i):
                sums[u] += weighted(keys, values, pl.multiple_of(i * tok, tok), tok, query_out[u])


def observed_part(packed, views, obs):
    sources, rows, tok = packed.shape
    span = sources // 2 * tok
    return pl.pallas_call(
        observed_kernel,
        out_shape=[
            jax.ShapeDtypeStruct((views, KEY_COLS, span), BF16),
            jax.ShapeDtypeStruct((views, VALUE_ROWS, span), F32),
        ],
        scratch_shapes=[
            pltpu.VMEM((obs * span, KEY_COLS), BF16),
            pltpu.VMEM((VALUE_ROWS, obs * span), BF16),
        ],
        compiler_params=params(40),
        cost_estimate=cost(8 * views * obs * span * span * HEAD_DIM, 4 * MIB),
        name="observed_part",
    )(packed)


def generated_kernel(view_set, query, before, packed, out, keys, values, sums, pairs):
    patches = packed.shape[0] // 2
    tok = packed.shape[2]
    views = query.shape[0]
    here = views // 2
    span = patches * tok
    count = jnp.int32(0)
    for u in range(views):
        for w in range(views):
            pairs[count] = u * views + w
            count = count + (view_set[u] == view_set[w]).astype(jnp.int32)
    for w in range(views):
        k_rows = slice((w % here) * HEAD_DIM, (w % here + 1) * HEAD_DIM)
        v_rows = slice((here + w % here) * HEAD_DIM, (here + w % here + 1) * HEAD_DIM)
        for p in range(patches):
            at = (w * patches + p) * tok
            store_keys(keys, at, packed[(w // here) * patches + p, k_rows, :])
            values[0:HEAD_DIM, at : at + tok] = packed[(w // here) * patches + p, v_rows, :]
    values[HEAD_DIM:, :] = jnp.ones((VALUE_ROWS - HEAD_DIM, views * span), BF16)
    sums[...] = before[...]

    def one_pair(i):
        u = pairs[i] // views
        start = pl.multiple_of((pairs[i] % views) * span, span)
        return u, weighted(keys, values, start, span, query[u])

    @pl.loop(0, count // 2)
    def _(i):
        u0, term0 = one_pair(2 * i)
        u1, term1 = one_pair(2 * i + 1)
        sums[u0] += term0
        sums[u1] += term1

    largest = jnp.max(sums[:, SUM_ROW : SUM_ROW + 1, :])

    @pl.when(jnp.logical_not(largest < LIMIT))
    def _():
        @pl.loop(0, views)
        def _(u):
            rows = -query[u, HEAD_DIM : HEAD_DIM + 16, :].astype(F32)
            old = rows[0:1] + rows[1:2] + rows[2:3]
            plain = jnp.concatenate(
                [query[u, 0:HEAD_DIM, :], jnp.zeros((KEY_COLS - HEAD_DIM, span), BF16)], axis=0
            )

            def look(w, top):
                seen = jnp.where(view_set[u] == view_set[w], span, 0)
                return block_max(keys, w * span, seen, tok, plain, top)

            top = lax.fori_loop(0, views, look, old)
            shifted = jnp.concatenate([query[u, 0:HEAD_DIM, :], offset_rows(top)], axis=0)
            sums[u] = before[u] * jnp.exp(old - top)

            @pl.loop(0, views)
            def _(w):
                @pl.when(view_set[u] == view_set[w])
                def _():
                    @pl.loop(0, patches)
                    def _(p):
                        start = pl.multiple_of(w * span + p * tok, tok)
                        sums[u] += weighted(keys, values, start, tok, shifted)

    for u in range(views):
        total = sums[u]
        context = (total[0:HEAD_DIM] / total[SUM_ROW : SUM_ROW + 1]).astype(BF16)
        rows = slice((u % here) * HEAD_DIM, (u % here + 1) * HEAD_DIM)
        for p in range(patches):
            out[(u // here) * patches + p, rows, :] = context[:, p * tok : (p + 1) * tok]


def generated_part(view_set, query, before, packed):
    sources, rows, tok = packed.shape
    views, _, span = query.shape
    vmem = pl.BlockSpec(memory_space=pltpu.VMEM)
    return pl.pallas_call(
        generated_kernel,
        in_specs=[pl.BlockSpec(memory_space=pltpu.SMEM), vmem, vmem, vmem],
        out_shape=jax.ShapeDtypeStruct((sources, rows // 2, tok), BF16),
        scratch_shapes=[
            pltpu.VMEM((views * span, KEY_COLS), BF16),
            pltpu.VMEM((VALUE_ROWS, views * span), BF16),
            pltpu.VMEM((views, VALUE_ROWS, span), F32),
            pltpu.SMEM((views * views + 1,), jnp.int32),
        ],
        compiler_params=params(40),
        cost_estimate=cost(6 * views * views * span * span * HEAD_DIM, 4 * MIB),
        name="generated_part",
    )(view_set, query, before, packed)


def project_out_kernel(packed, weight, out, context):
    views, tok = out.shape[:2]

    @pl.when(pl.program_id(0) == 0)
    def _():
        for i in range(views):
            rows = packed[:, i * HEAD_DIM : (i + 1) * HEAD_DIM, :].reshape(HEADS * HEAD_DIM, tok)
            context[i * tok : (i + 1) * tok, :] = rows.T

    out[...] = dot(context[...], weight[...]).astype(BF16).reshape(out.shape)


def project_out(packed, weight):
    heads, rows, tok = packed.shape
    views = rows // HEAD_DIM
    width = weight.shape[0]
    steps = 2
    cols = width // steps
    return pl.pallas_call(
        project_out_kernel,
        grid=(steps,),
        in_specs=[
            pl.BlockSpec((heads, rows, tok), lambda j: (0, 0, 0)),
            pl.BlockSpec((width, cols), lambda j: (0, j)),
        ],
        out_specs=pl.BlockSpec((views, tok, cols), lambda j: (0, 0, j)),
        out_shape=jax.ShapeDtypeStruct((views, tok, width), BF16),
        scratch_shapes=[pltpu.VMEM((views * tok, width), BF16)],
        compiler_params=params(24),
        cost_estimate=cost(2 * views * tok * width * width, 4 * MIB),
        name="project_out",
    )(packed, weight)


def exchange(blocks):
    return lax.all_to_all(blocks, ("view", "patch"), split_axis=0, concat_axis=0, tiled=True)


def on_device(hidden, rays, view_set, obs_keys, obs_values, w_query, w_key, w_value, w_out):
    views = view_set.shape[0]
    view = lax.axis_index("view").astype(jnp.int32).reshape(1)
    queries = exchange(pack_queries(view, hidden, rays, w_query, obs_keys, obs_values))
    pairs = exchange(pack_pairs(hidden, rays, w_key, w_value))
    query, before = observed_part(queries, views, obs_keys.shape[0])
    context = exchange(generated_part(view_set, query, before, pairs))
    return project_out(context, w_out)


def solution(mesh):
    return jax.shard_map(
        on_device,
        mesh=mesh,
        in_specs=(
            P(("group", "view"), "patch", None),
            P(("group", "view"), "patch", None),
            P("group"),
            P(None, "patch", None),
            P(None, "patch", None),
            P(),
            P(),
            P(),
            P(),
        ),
        out_specs=P(("group", "view"), "patch", None),
        check_vma=False,
    )
```

```python
import jax
import jax.numpy as jnp
from jax import lax
from jax.experimental import pallas as pl
from jax.experimental.pallas import tpu as pltpu
from jax.sharding import PartitionSpec as P

HEADS = 16
HEAD_DIM = 64
SUM_ROW = HEAD_DIM
VALUE_ROWS = HEAD_DIM + 16
KEY_COLS = 2 * HEAD_DIM
LIMIT = 2.0**100
BF16 = jnp.bfloat16
F32 = jnp.float32
MIB = 2**20


def dot(a, b):
    return jnp.dot(a, b, preferred_element_type=F32)


def params(mib):
    return pltpu.CompilerParams(vmem_limit_bytes=mib * MIB)


def cost(flops, nbytes):
    return pl.CostEstimate(flops=int(flops), bytes_accessed=int(nbytes), transcendentals=0)


def pack_kernel(
    view, hidden, rays, w_query, w_key, w_value, obs_k, obs_v, queries, pairs,
    hid, ray, weights, obs, source, query_blocks, pair_blocks, in_sem, out_sem,
):
    views, tok = hidden.shape[:2]
    copies = [pltpu.make_async_copy(hidden, hid, in_sem.at[0]), pltpu.make_async_copy(rays, ray, in_sem.at[1])]
    loads = [
        pltpu.make_async_copy(w, weights.at[i], in_sem.at[2 + i]) for i, w in enumerate((w_query, w_key, w_value))
    ]
    observed = [pltpu.make_async_copy(o, obs, in_sem.at[5]) for o in (obs_k, obs_v)]
    for c in copies:
        c.start()
    loads[0].start()
    for kind in range(2):

        @pl.when(view[0] == kind)
        def _():
            observed[kind].start()

    for c in loads[1:]:
        c.start()
    for c in copies:
        c.wait()
    both = hid[...].astype(F32) + ray[...].astype(F32)
    source[...] = both.astype(BF16).reshape(source.shape)

    def place(blocks, base, feats, count):
        for head in range(HEADS):
            rows = slice(head * HEAD_DIM, (head + 1) * HEAD_DIM)
            for i in range(count):
                at = (base + i) * HEAD_DIM
                blocks[head, at : at + HEAD_DIM, :] = feats[rows, i * tok : (i + 1) * tok]

    def feats_of(i):
        loads[i].wait()
        return dot(source[...], weights[i]).astype(BF16)

    place(query_blocks, 0, (feats_of(0) * jnp.asarray(HEAD_DIM**-0.5, BF16)).T, views)
    observed[0].wait()
    place(query_blocks, views, obs[...].reshape(-1, obs.shape[-1]).T, obs.shape[0])
    sends = [pltpu.make_async_copy(query_blocks, queries, out_sem.at[0])]
    sends[0].start()
    place(pair_blocks, 0, feats_of(1).T, views)
    place(pair_blocks, views, feats_of(2).T, views)
    sends.append(pltpu.make_async_copy(pair_blocks, pairs, out_sem.at[1]))
    sends[1].start()
    for c in sends:
        c.wait()


def pack(view, hidden, rays, w_query, w_key, w_value, obs_k, obs_v):
    views, tok, width = hidden.shape
    query_shape = (HEADS, (views + obs_k.shape[0]) * HEAD_DIM, tok)
    pair_shape = (HEADS, 2 * views * HEAD_DIM, tok)
    hbm = pl.BlockSpec(memory_space=pltpu.MemorySpace.HBM)
    return pl.pallas_call(
        pack_kernel,
        in_specs=[pl.BlockSpec(memory_space=pltpu.SMEM)] + [hbm] * 7,
        out_specs=[hbm, hbm],
        out_shape=[jax.ShapeDtypeStruct(query_shape, BF16), jax.ShapeDtypeStruct(pair_shape, BF16)],
        scratch_shapes=[
            pltpu.VMEM(hidden.shape, BF16),
            pltpu.VMEM(rays.shape, BF16),
            pltpu.VMEM((3,) + w_query.shape, BF16),
            pltpu.VMEM(obs_k.shape, BF16),
            pltpu.VMEM((views * tok, width), BF16),
            pltpu.VMEM(query_shape, BF16),
            pltpu.VMEM(pair_shape, BF16),
            pltpu.SemaphoreType.DMA((6,)),
            pltpu.SemaphoreType.DMA((2,)),
        ],
        compiler_params=params(56),
        cost_estimate=cost(6 * views * tok * width * width, 10 * MIB),
        name="pack",
    )(view, hidden, rays, w_query, w_key, w_value, obs_k, obs_v)


def ones_rows(count, ones, lanes):
    row = lax.broadcasted_iota(jnp.int32, (count, lanes), 0)
    return jnp.where(row < ones, 1.0, 0.0).astype(BF16)


def store_keys(keys, at, turned):
    tok = turned.shape[1]
    full = jnp.concatenate([turned, ones_rows(KEY_COLS - HEAD_DIM, 3, tok)], axis=0)
    keys[at : at + tok, :] = full.T


def offset_rows(top):
    first = top.astype(BF16)
    rest = top - first.astype(F32)
    second = rest.astype(BF16)
    third = rest - second.astype(F32)
    row = lax.broadcasted_iota(jnp.int32, (KEY_COLS - HEAD_DIM, top.shape[1]), 0)
    picked = jnp.where(row == 0, first.astype(F32), 0.0)
    picked = jnp.where(row == 1, second.astype(F32), picked)
    picked = jnp.where(row == 2, third, picked)
    return (-picked).astype(BF16)


def block_max(keys, at, count, block, query, top):
    def step(i, top):
        start = pl.multiple_of(at + i * block, block)
        scores = dot(keys[pl.ds(start, block), :], query)
        return jnp.maximum(top, jnp.max(scores, axis=0, keepdims=True))

    return lax.fori_loop(0, count // block, step, top)


def weighted(keys, values, start, count, query):
    weights = jnp.exp(dot(keys[pl.ds(start, count), :], query)).astype(BF16)
    return dot(values[:, pl.ds(start, count)], weights)


def observed_kernel(packed, query_out, sums_out, keys, values, sums, sems):
    patches = packed.shape[0] // 2
    tok = packed.shape[2]
    views = query_out.shape[0]
    here = views // 2
    obs = packed.shape[1] // HEAD_DIM - here
    span = patches * tok
    for o in range(obs):
        rows = slice((here + o) * HEAD_DIM, (here + o + 1) * HEAD_DIM)
        for p in range(patches):
            at = (o * patches + p) * tok
            store_keys(keys, at, packed[p, rows, :])
            values[0:HEAD_DIM, at : at + tok] = packed[patches + p, rows, :]
    values[HEAD_DIM:, :] = jnp.ones((VALUE_ROWS - HEAD_DIM, obs * span), BF16)
    for u in range(views):
        rows = slice((u % here) * HEAD_DIM, (u % here + 1) * HEAD_DIM)
        query = jnp.concatenate([packed[(u // here) * patches + p, rows, :] for p in range(patches)], axis=1)
        query_out[u, 0:HEAD_DIM, :] = query
        top = jnp.max(dot(keys[0:tok, 0:HEAD_DIM], query), axis=0, keepdims=True)
        query_out[u, HEAD_DIM:, :] = offset_rows(top)

    def one_view(u, block):
        query = query_out[u]
        total = None
        for o in range(obs * span // block):
            term = weighted(keys, values, o * block, block, query)
            total = term if total is None else total + term
        sums[u] = total

    def send(u):
        return pltpu.make_async_copy(sums.at[u], sums_out.at[u], sems.at[u])

    @pl.loop(0, views)
    def _(u):
        one_view(u, span)
        send(u).start()

    largest = jnp.max(sums[:, SUM_ROW : SUM_ROW + 1, :])
    for u in range(views):
        send(u).wait()

    @pl.when(jnp.logical_not(largest < LIMIT))
    def _():
        @pl.loop(0, views)
        def _(u):
            query_out[u, HEAD_DIM:, :] = jnp.zeros((KEY_COLS - HEAD_DIM, span), BF16)
            low = jnp.full((1, span), -jnp.inf, F32)
            top = block_max(keys, 0, obs * span, tok, query_out[u], low)
            query_out[u, HEAD_DIM:, :] = offset_rows(top)
            sums[u] = jnp.zeros(sums.shape[1:], F32)

            @pl.loop(0, obs * patches)
            def _(i):
                sums[u] += weighted(keys, values, pl.multiple_of(i * tok, tok), tok, query_out[u])

            send(u).start()
            send(u).wait()


def observed_part(packed, views, obs):
    sources, rows, tok = packed.shape
    span = sources // 2 * tok
    vmem = pl.BlockSpec(memory_space=pltpu.VMEM)
    return pl.pallas_call(
        observed_kernel,
        in_specs=[vmem],
        out_specs=[vmem, pl.BlockSpec(memory_space=pltpu.MemorySpace.HBM)],
        out_shape=[
            jax.ShapeDtypeStruct((views, KEY_COLS, span), BF16),
            pltpu.MemorySpace.HBM((views, VALUE_ROWS, span), F32),
        ],
        scratch_shapes=[
            pltpu.VMEM((obs * span, KEY_COLS), BF16),
            pltpu.VMEM((VALUE_ROWS, obs * span), BF16),
            pltpu.VMEM((views, VALUE_ROWS, span), F32),
            pltpu.SemaphoreType.DMA((views,)),
        ],
        compiler_params=params(32),
        cost_estimate=cost(8 * views * obs * span * span * HEAD_DIM, 4 * MIB),
        name="observed_part",
    )(packed)


def generated_kernel(view_set, query, before, packed, out, keys, values, sums, pairs, sem):
    patches = packed.shape[0] // 2
    tok = packed.shape[2]
    views = query.shape[0]
    here = views // 2
    span = patches * tok
    fetch = pltpu.make_async_copy(before, sums, sem)
    fetch.start()
    count = jnp.int32(0)
    for u in range(views):
        for w in range(views):
            pairs[count] = u * views + w
            count = count + (view_set[u] == view_set[w]).astype(jnp.int32)
    for w in range(views):
        k_rows = slice((w % here) * HEAD_DIM, (w % here + 1) * HEAD_DIM)
        v_rows = slice((here + w % here) * HEAD_DIM, (here + w % here + 1) * HEAD_DIM)
        for p in range(patches):
            at = (w * patches + p) * tok
            store_keys(keys, at, packed[(w // here) * patches + p, k_rows, :])
            values[0:HEAD_DIM, at : at + tok] = packed[(w // here) * patches + p, v_rows, :]
    values[HEAD_DIM:, :] = jnp.ones((VALUE_ROWS - HEAD_DIM, views * span), BF16)
    fetch.wait()

    def one_pair(i):
        u = pairs[i] // views
        start = pl.multiple_of((pairs[i] % views) * span, span)
        return u, weighted(keys, values, start, span, query[u])

    @pl.loop(0, count // 2)
    def _(i):
        u0, term0 = one_pair(2 * i)
        u1, term1 = one_pair(2 * i + 1)
        sums[u0] += term0
        sums[u1] += term1

    largest = jnp.max(sums[:, SUM_ROW : SUM_ROW + 1, :])

    @pl.when(jnp.logical_not(largest < LIMIT))
    def _():
        again = pltpu.make_async_copy(before, sums, sem)
        again.start()
        again.wait()

        @pl.loop(0, views)
        def _(u):
            rows = -query[u, HEAD_DIM : HEAD_DIM + 16, :].astype(F32)
            old = rows[0:1] + rows[1:2] + rows[2:3]
            plain = jnp.concatenate(
                [query[u, 0:HEAD_DIM, :], jnp.zeros((KEY_COLS - HEAD_DIM, span), BF16)], axis=0
            )

            def look(w, top):
                seen = jnp.where(view_set[u] == view_set[w], span, 0)
                return block_max(keys, w * span, seen, tok, plain, top)

            top = lax.fori_loop(0, views, look, old)
            shifted = jnp.concatenate([query[u, 0:HEAD_DIM, :], offset_rows(top)], axis=0)
            sums[u] = sums[u] * jnp.exp(old - top)

            @pl.loop(0, views)
            def _(w):
                @pl.when(view_set[u] == view_set[w])
                def _():
                    @pl.loop(0, patches)
                    def _(p):
                        start = pl.multiple_of(w * span + p * tok, tok)
                        sums[u] += weighted(keys, values, start, tok, shifted)

    for u in range(views):
        total = sums[u]
        context = (total[0:HEAD_DIM] / total[SUM_ROW : SUM_ROW + 1]).astype(BF16)
        rows = slice((u % here) * HEAD_DIM, (u % here + 1) * HEAD_DIM)
        for p in range(patches):
            out[(u // here) * patches + p, rows, :] = context[:, p * tok : (p + 1) * tok]


def generated_part(view_set, query, before, packed):
    sources, rows, tok = packed.shape
    views, _, span = query.shape
    vmem = pl.BlockSpec(memory_space=pltpu.VMEM)
    return pl.pallas_call(
        generated_kernel,
        in_specs=[
            pl.BlockSpec(memory_space=pltpu.SMEM),
            vmem,
            pl.BlockSpec(memory_space=pltpu.MemorySpace.HBM),
            vmem,
        ],
        out_specs=vmem,
        out_shape=jax.ShapeDtypeStruct((sources, rows // 2, tok), BF16),
        scratch_shapes=[
            pltpu.VMEM((views * span, KEY_COLS), BF16),
            pltpu.VMEM((VALUE_ROWS, views * span), BF16),
            pltpu.VMEM((views, VALUE_ROWS, span), F32),
            pltpu.SMEM((views * views + 1,), jnp.int32),
            pltpu.SemaphoreType.DMA,
        ],
        compiler_params=params(32),
        cost_estimate=cost(6 * views * views * span * span * HEAD_DIM, 4 * MIB),
        name="generated_part",
    )(view_set, query, pltpu.with_memory_space_constraint(before, pltpu.MemorySpace.HBM), packed)


def project_out_kernel(packed, weight, out, context, blocks, sems):
    views, tok = out.shape[:2]
    for i in range(views):
        rows = packed[:, i * HEAD_DIM : (i + 1) * HEAD_DIM, :].reshape(HEADS * HEAD_DIM, tok)
        context[i * tok : (i + 1) * tok, :] = rows.T
    copies = []
    cols = weight.shape[1] // 2
    for j in range(2):
        at = slice(j * cols, (j + 1) * cols)
        blocks[:, :, at] = dot(context[...], weight[:, at]).astype(BF16).reshape(views, tok, cols)
        copies.append(pltpu.make_async_copy(blocks.at[:, :, at], out.at[:, :, at], sems.at[j]))
        copies[j].start()
    for c in copies:
        c.wait()


def project_out(packed, weight):
    heads, rows, tok = packed.shape
    views = rows // HEAD_DIM
    width = weight.shape[0]
    vmem = pl.BlockSpec(memory_space=pltpu.VMEM)
    return pl.pallas_call(
        project_out_kernel,
        in_specs=[vmem, vmem],
        out_specs=pl.BlockSpec(memory_space=pltpu.MemorySpace.HBM),
        out_shape=jax.ShapeDtypeStruct((views, tok, width), BF16),
        scratch_shapes=[
            pltpu.VMEM((views * tok, width), BF16),
            pltpu.VMEM((views, tok, width), BF16),
            pltpu.SemaphoreType.DMA((2,)),
        ],
        compiler_params=params(24),
        cost_estimate=cost(2 * views * tok * width * width, 4 * MIB),
        name="project_out",
    )(packed, weight)


def exchange(blocks):
    return lax.all_to_all(blocks, ("view", "patch"), split_axis=0, concat_axis=0, tiled=True)


def on_device(hidden, rays, view_set, obs_keys, obs_values, w_query, w_key, w_value, w_out):
    views = view_set.shape[0]
    view = lax.axis_index("view").astype(jnp.int32).reshape(1)
    queries, pairs = pack(view, hidden, rays, w_query, w_key, w_value, obs_keys, obs_values)
    queries = exchange(queries)
    pairs = exchange(pairs)
    query, before = observed_part(queries, views, obs_keys.shape[0])
    context = exchange(generated_part(view_set, query, before, pairs))
    return project_out(context, w_out)


def solution(mesh):
    return jax.shard_map(
        on_device,
        mesh=mesh,
        in_specs=(
            P(("group", "view"), "patch", None),
            P(("group", "view"), "patch", None),
            P("group"),
            P(None, "patch", None),
            P(None, "patch", None),
            P(),
            P(),
            P(),
            P(),
        ),
        out_specs=P(("group", "view"), "patch", None),
        check_vma=False,
    )
```

```python
import jax
import jax.numpy as jnp
from jax import lax
from jax.experimental import pallas as pl
from jax.experimental.pallas import tpu as pltpu
from jax.sharding import PartitionSpec as P

HEADS = 16
HEAD_DIM = 64
SUM_ROW = HEAD_DIM
VALUE_ROWS = HEAD_DIM + 16
KEY_COLS = 2 * HEAD_DIM
LIMIT = 2.0**100
BF16 = jnp.bfloat16
F32 = jnp.float32
MIB = 2**20


def dot(a, b):
    return jnp.dot(a, b, preferred_element_type=F32)


def params(mib):
    return pltpu.CompilerParams(vmem_limit_bytes=mib * MIB)


def cost(flops, nbytes):
    return pl.CostEstimate(flops=int(flops), bytes_accessed=int(nbytes), transcendentals=0)


HBM = pl.BlockSpec(memory_space=pltpu.MemorySpace.HBM)
COLUMNS = 2


def column_loads(weight, held, sems, first):
    cols = weight.shape[1] // COLUMNS
    return [
        pltpu.make_async_copy(
            weight.at[:, j * cols : (j + 1) * cols], held.at[:, j * cols : (j + 1) * cols], sems.at[first + j]
        )
        for j in range(COLUMNS)
    ]


def make_source(hid, ray, source):
    both = hid[...].astype(F32) + ray[...].astype(F32)
    source[...] = both.astype(BF16).reshape(source.shape)


def place(blocks, first, base, feats, count, tok):
    for head in range(feats.shape[0] // HEAD_DIM):
        rows = slice(head * HEAD_DIM, (head + 1) * HEAD_DIM)
        for i in range(count):
            at = (base + i) * HEAD_DIM
            blocks[first + head, at : at + HEAD_DIM, :] = feats[rows, i * tok : (i + 1) * tok]


def pack_queries_kernel(
    view, hidden, rays, weight, obs_k, obs_v, out, hid, ray, held, obs, source, blocks, in_sem, out_sem
):
    views, tok = hidden.shape[:2]
    inputs = [pltpu.make_async_copy(hidden, hid, in_sem.at[0]), pltpu.make_async_copy(rays, ray, in_sem.at[1])]
    observed = [pltpu.make_async_copy(o, obs, in_sem.at[2]) for o in (obs_k, obs_v)]
    columns = column_loads(weight, held, in_sem, 3)
    for kind in range(2):

        @pl.when(view[0] == kind)
        def _():
            observed[kind].start()

    for c in inputs + columns:
        c.start()
    base = views * HEAD_DIM
    sends = []

    def send(place_of):
        sends.append(pltpu.make_async_copy(blocks.at[place_of], out.at[place_of], out_sem.at[len(sends)]))
        sends[-1].start()

    observed[0].wait()
    place(blocks, 0, views, obs[...].reshape(-1, obs.shape[-1]).T, obs.shape[0], tok)
    send((slice(None), slice(base, None)))
    for c in inputs:
        c.wait()
    make_source(hid, ray, source)
    cols = weight.shape[1] // COLUMNS
    heads = HEADS // COLUMNS
    for j in range(COLUMNS):
        columns[j].wait()
        feats = dot(source[...], held[:, j * cols : (j + 1) * cols]).astype(BF16) * jnp.asarray(HEAD_DIM**-0.5, BF16)
        place(blocks, j * heads, 0, feats.T, views, tok)
        send((slice(j * heads, (j + 1) * heads), slice(0, base)))
    for c in sends:
        c.wait()


def pack_queries(view, hidden, rays, weight, obs_k, obs_v):
    views, tok, width = hidden.shape
    shape = (HEADS, (views + obs_k.shape[0]) * HEAD_DIM, tok)
    return pl.pallas_call(
        pack_queries_kernel,
        in_specs=[pl.BlockSpec(memory_space=pltpu.SMEM)] + [HBM] * 5,
        out_specs=HBM,
        out_shape=jax.ShapeDtypeStruct(shape, BF16),
        scratch_shapes=[
            pltpu.VMEM(hidden.shape, BF16),
            pltpu.VMEM(rays.shape, BF16),
            pltpu.VMEM(weight.shape, BF16),
            pltpu.VMEM(obs_k.shape, BF16),
            pltpu.VMEM((views * tok, width), BF16),
            pltpu.VMEM(shape, BF16),
            pltpu.SemaphoreType.DMA((3 + COLUMNS,)),
            pltpu.SemaphoreType.DMA((1 + COLUMNS,)),
        ],
        compiler_params=params(58),
        cost_estimate=cost(2 * views * tok * width * width, 6 * MIB),
        name="pack_queries",
    )(view, hidden, rays, weight, obs_k, obs_v)


def pack_pairs_kernel(hidden, rays, w_key, w_value, out, hid, ray, held_k, held_v, source, blocks, in_sem, out_sem):
    views, tok = hidden.shape[:2]
    inputs = [pltpu.make_async_copy(hidden, hid, in_sem.at[0]), pltpu.make_async_copy(rays, ray, in_sem.at[1])]
    columns = column_loads(w_key, held_k, in_sem, 2) + column_loads(w_value, held_v, in_sem, 2 + COLUMNS)
    for c in inputs + columns:
        c.start()
    for c in inputs:
        c.wait()
    make_source(hid, ray, source)
    cols = w_key.shape[1] // COLUMNS
    heads = HEADS // COLUMNS
    for i, held in enumerate((held_k, held_v)):
        for j in range(COLUMNS):
            columns[i * COLUMNS + j].wait()
            feats = dot(source[...], held[:, j * cols : (j + 1) * cols]).astype(BF16)
            place(blocks, j * heads, i * views, feats.T, views, tok)
    send = pltpu.make_async_copy(blocks, out, out_sem)
    send.start()
    send.wait()


def pack_pairs(hidden, rays, w_key, w_value):
    views, tok, width = hidden.shape
    shape = (HEADS, 2 * views * HEAD_DIM, tok)
    return pl.pallas_call(
        pack_pairs_kernel,
        in_specs=[HBM] * 4,
        out_specs=HBM,
        out_shape=jax.ShapeDtypeStruct(shape, BF16),
        scratch_shapes=[
            pltpu.VMEM(hidden.shape, BF16),
            pltpu.VMEM(rays.shape, BF16),
            pltpu.VMEM(w_key.shape, BF16),
            pltpu.VMEM(w_value.shape, BF16),
            pltpu.VMEM((views * tok, width), BF16),
            pltpu.VMEM(shape, BF16),
            pltpu.SemaphoreType.DMA((2 + 2 * COLUMNS,)),
            pltpu.SemaphoreType.DMA,
        ],
        compiler_params=params(58),
        cost_estimate=cost(4 * views * tok * width * width, 7 * MIB),
        name="pack_pairs",
    )(hidden, rays, w_key, w_value)


def ones_rows(count, ones, lanes):
    row = lax.broadcasted_iota(jnp.int32, (count, lanes), 0)
    return jnp.where(row < ones, 1.0, 0.0).astype(BF16)


def store_keys(keys, at, turned):
    tok = turned.shape[1]
    full = jnp.concatenate([turned, ones_rows(KEY_COLS - HEAD_DIM, 3, tok)], axis=0)
    keys[at : at + tok, :] = full.T


def offset_rows(top):
    first = top.astype(BF16)
    rest = top - first.astype(F32)
    second = rest.astype(BF16)
    third = rest - second.astype(F32)
    row = lax.broadcasted_iota(jnp.int32, (KEY_COLS - HEAD_DIM, top.shape[1]), 0)
    picked = jnp.where(row == 0, first.astype(F32), 0.0)
    picked = jnp.where(row == 1, second.astype(F32), picked)
    picked = jnp.where(row == 2, third, picked)
    return (-picked).astype(BF16)


def block_max(keys, at, count, block, query, top):
    def step(i, top):
        start = pl.multiple_of(at + i * block, block)
        scores = dot(keys[pl.ds(start, block), :], query)
        return jnp.maximum(top, jnp.max(scores, axis=0, keepdims=True))

    return lax.fori_loop(0, count // block, step, top)


def weighted(keys, values, start, count, query):
    weights = jnp.exp(dot(keys[pl.ds(start, count), :], query)).astype(BF16)
    return dot(values[:, pl.ds(start, count)], weights)


def observed_kernel(packed, query_out, sums_out, keys, values, sums, sems):
    patches = packed.shape[0] // 2
    tok = packed.shape[2]
    views = query_out.shape[0]
    here = views // 2
    obs = packed.shape[1] // HEAD_DIM - here
    span = patches * tok
    for o in range(obs):
        rows = slice((here + o) * HEAD_DIM, (here + o + 1) * HEAD_DIM)
        for p in range(patches):
            at = (o * patches + p) * tok
            store_keys(keys, at, packed[p, rows, :])
            values[0:HEAD_DIM, at : at + tok] = packed[patches + p, rows, :]
    values[HEAD_DIM:, :] = jnp.ones((VALUE_ROWS - HEAD_DIM, obs * span), BF16)
    for u in range(views):
        rows = slice((u % here) * HEAD_DIM, (u % here + 1) * HEAD_DIM)
        query = jnp.concatenate([packed[(u // here) * patches + p, rows, :] for p in range(patches)], axis=1)
        query_out[u, 0:HEAD_DIM, :] = query
        top = jnp.max(dot(keys[0:tok, 0:HEAD_DIM], query), axis=0, keepdims=True)
        query_out[u, HEAD_DIM:, :] = offset_rows(top)

    def one_view(u, block):
        query = query_out[u]
        total = None
        for o in range(obs * span // block):
            term = weighted(keys, values, o * block, block, query)
            total = term if total is None else total + term
        sums[u] = total

    def send(u):
        return pltpu.make_async_copy(sums.at[u], sums_out.at[u], sems.at[u])

    @pl.loop(0, views)
    def _(u):
        one_view(u, span)
        send(u).start()

    largest = jnp.max(sums[:, SUM_ROW : SUM_ROW + 1, :])
    for u in range(views):
        send(u).wait()

    @pl.when(jnp.logical_not(largest < LIMIT))
    def _():
        @pl.loop(0, views)
        def _(u):
            query_out[u, HEAD_DIM:, :] = jnp.zeros((KEY_COLS - HEAD_DIM, span), BF16)
            low = jnp.full((1, span), -jnp.inf, F32)
            top = block_max(keys, 0, obs * span, tok, query_out[u], low)
            query_out[u, HEAD_DIM:, :] = offset_rows(top)
            sums[u] = jnp.zeros(sums.shape[1:], F32)

            @pl.loop(0, obs * patches)
            def _(i):
                sums[u] += weighted(keys, values, pl.multiple_of(i * tok, tok), tok, query_out[u])

            send(u).start()
            send(u).wait()


def observed_part(packed, views, obs):
    sources, rows, tok = packed.shape
    span = sources // 2 * tok
    vmem = pl.BlockSpec(memory_space=pltpu.VMEM)
    return pl.pallas_call(
        observed_kernel,
        in_specs=[vmem],
        out_specs=[vmem, pl.BlockSpec(memory_space=pltpu.MemorySpace.HBM)],
        out_shape=[
            jax.ShapeDtypeStruct((views, KEY_COLS, span), BF16),
            pltpu.MemorySpace.HBM((views, VALUE_ROWS, span), F32),
        ],
        scratch_shapes=[
            pltpu.VMEM((obs * span, KEY_COLS), BF16),
            pltpu.VMEM((VALUE_ROWS, obs * span), BF16),
            pltpu.VMEM((views, VALUE_ROWS, span), F32),
            pltpu.SemaphoreType.DMA((views,)),
        ],
        compiler_params=params(32),
        cost_estimate=cost(8 * views * obs * span * span * HEAD_DIM, 4 * MIB),
        name="observed_part",
    )(packed)


def generated_kernel(view_set, query, before, packed, out, keys, values, sums, pairs, early, sem):
    patches = packed.shape[0] // 2
    tok = packed.shape[2]
    views = query.shape[0]
    here = views // 2
    span = patches * tok
    fetch = pltpu.make_async_copy(before, early, sem)
    fetch.start()
    count = jnp.int32(0)
    for u in range(views):
        for w in range(views):
            pairs[count] = u * views + w
            count = count + (view_set[u] == view_set[w]).astype(jnp.int32)
    for w in range(views):
        k_rows = slice((w % here) * HEAD_DIM, (w % here + 1) * HEAD_DIM)
        v_rows = slice((here + w % here) * HEAD_DIM, (here + w % here + 1) * HEAD_DIM)
        for p in range(patches):
            at = (w * patches + p) * tok
            store_keys(keys, at, packed[(w // here) * patches + p, k_rows, :])
            values[0:HEAD_DIM, at : at + tok] = packed[(w // here) * patches + p, v_rows, :]
    values[HEAD_DIM:, :] = jnp.ones((VALUE_ROWS - HEAD_DIM, views * span), BF16)
    sums[...] = jnp.zeros(sums.shape, F32)

    def one_pair(i):
        u = pairs[i] // views
        start = pl.multiple_of((pairs[i] % views) * span, span)
        return u, weighted(keys, values, start, span, query[u])

    @pl.loop(0, count // 2)
    def _(i):
        u0, term0 = one_pair(2 * i)
        u1, term1 = one_pair(2 * i + 1)
        sums[u0] += term0
        sums[u1] += term1

    largest = jnp.max(sums[:, SUM_ROW : SUM_ROW + 1, :])
    fetch.wait()

    @pl.when(jnp.logical_not(largest < LIMIT))
    def _():
        @pl.loop(0, views)
        def _(u):
            rows = -query[u, HEAD_DIM : HEAD_DIM + 16, :].astype(F32)
            old = rows[0:1] + rows[1:2] + rows[2:3]
            plain = jnp.concatenate(
                [query[u, 0:HEAD_DIM, :], jnp.zeros((KEY_COLS - HEAD_DIM, span), BF16)], axis=0
            )

            def look(w, top):
                seen = jnp.where(view_set[u] == view_set[w], span, 0)
                return block_max(keys, w * span, seen, tok, plain, top)

            top = lax.fori_loop(0, views, look, old)
            shifted = jnp.concatenate([query[u, 0:HEAD_DIM, :], offset_rows(top)], axis=0)
            early[u] = early[u] * jnp.exp(old - top)
            sums[u] = jnp.zeros(sums.shape[1:], F32)

            @pl.loop(0, views)
            def _(w):
                @pl.when(view_set[u] == view_set[w])
                def _():
                    @pl.loop(0, patches)
                    def _(p):
                        start = pl.multiple_of(w * span + p * tok, tok)
                        sums[u] += weighted(keys, values, start, tok, shifted)

    for u in range(views):
        total = sums[u] + early[u]
        context = (total[0:HEAD_DIM] / total[SUM_ROW : SUM_ROW + 1]).astype(BF16)
        rows = slice((u % here) * HEAD_DIM, (u % here + 1) * HEAD_DIM)
        for p in range(patches):
            out[(u // here) * patches + p, rows, :] = context[:, p * tok : (p + 1) * tok]


def generated_part(view_set, query, before, packed):
    sources, rows, tok = packed.shape
    views, _, span = query.shape
    vmem = pl.BlockSpec(memory_space=pltpu.VMEM)
    return pl.pallas_call(
        generated_kernel,
        in_specs=[
            pl.BlockSpec(memory_space=pltpu.SMEM),
            vmem,
            pl.BlockSpec(memory_space=pltpu.MemorySpace.HBM),
            vmem,
        ],
        out_specs=vmem,
        out_shape=jax.ShapeDtypeStruct((sources, rows // 2, tok), BF16),
        scratch_shapes=[
            pltpu.VMEM((views * span, KEY_COLS), BF16),
            pltpu.VMEM((VALUE_ROWS, views * span), BF16),
            pltpu.VMEM((views, VALUE_ROWS, span), F32),
            pltpu.SMEM((views * views + 1,), jnp.int32),
            pltpu.VMEM((views, VALUE_ROWS, span), F32),
            pltpu.SemaphoreType.DMA,
        ],
        compiler_params=params(32),
        cost_estimate=cost(6 * views * views * span * span * HEAD_DIM, 4 * MIB),
        name="generated_part",
    )(view_set, query, pltpu.with_memory_space_constraint(before, pltpu.MemorySpace.HBM), packed)


def project_out_kernel(packed, weight, out, context, blocks, sems):
    views, tok = out.shape[:2]
    for i in range(views):
        rows = packed[:, i * HEAD_DIM : (i + 1) * HEAD_DIM, :].reshape(HEADS * HEAD_DIM, tok)
        context[i * tok : (i + 1) * tok, :] = rows.T
    copies = []
    cols = weight.shape[1] // 2
    for j in range(2):
        at = slice(j * cols, (j + 1) * cols)
        blocks[:, :, at] = dot(context[...], weight[:, at]).astype(BF16).reshape(views, tok, cols)
        copies.append(pltpu.make_async_copy(blocks.at[:, :, at], out.at[:, :, at], sems.at[j]))
        copies[j].start()
    for c in copies:
        c.wait()


def project_out(packed, weight):
    heads, rows, tok = packed.shape
    views = rows // HEAD_DIM
    width = weight.shape[0]
    vmem = pl.BlockSpec(memory_space=pltpu.VMEM)
    return pl.pallas_call(
        project_out_kernel,
        in_specs=[vmem, vmem],
        out_specs=pl.BlockSpec(memory_space=pltpu.MemorySpace.HBM),
        out_shape=jax.ShapeDtypeStruct((views, tok, width), BF16),
        scratch_shapes=[
            pltpu.VMEM((views * tok, width), BF16),
            pltpu.VMEM((views, tok, width), BF16),
            pltpu.SemaphoreType.DMA((2,)),
        ],
        compiler_params=params(24),
        cost_estimate=cost(2 * views * tok * width * width, 4 * MIB),
        name="project_out",
    )(packed, weight)


def exchange(blocks):
    return lax.all_to_all(blocks, ("view", "patch"), split_axis=0, concat_axis=0, tiled=True)


def on_device(hidden, rays, view_set, obs_keys, obs_values, w_query, w_key, w_value, w_out):
    views = view_set.shape[0]
    view = lax.axis_index("view").astype(jnp.int32).reshape(1)
    queries = exchange(pack_queries(view, hidden, rays, w_query, obs_keys, obs_values))
    pairs = exchange(pack_pairs(hidden, rays, w_key, w_value))
    query, before = observed_part(queries, views, obs_keys.shape[0])
    context = exchange(generated_part(view_set, query, before, pairs))
    return project_out(context, w_out)


def solution(mesh):
    return jax.shard_map(
        on_device,
        mesh=mesh,
        in_specs=(
            P(("group", "view"), "patch", None),
            P(("group", "view"), "patch", None),
            P("group"),
            P(None, "patch", None),
            P(None, "patch", None),
            P(),
            P(),
            P(),
            P(),
        ),
        out_specs=P(("group", "view"), "patch", None),
        check_vma=False,
    )
```

```python
import jax
import jax.numpy as jnp
from jax import lax
from jax.experimental import pallas as pl
from jax.experimental.pallas import tpu as pltpu
from jax.sharding import PartitionSpec as P

HEADS = 16
HEAD_DIM = 64
SUM_ROW = HEAD_DIM
VALUE_ROWS = HEAD_DIM + 16
KEY_COLS = 2 * HEAD_DIM
LIMIT = 2.0**100
BF16 = jnp.bfloat16
F32 = jnp.float32
MIB = 2**20


def dot(a, b):
    return jnp.dot(a, b, preferred_element_type=F32)


def params(mib):
    return pltpu.CompilerParams(vmem_limit_bytes=mib * MIB)


def cost(flops, nbytes):
    return pl.CostEstimate(flops=int(flops), bytes_accessed=int(nbytes), transcendentals=0)


HBM = pl.BlockSpec(memory_space=pltpu.MemorySpace.HBM)
COLUMNS = 2


def column_loads(weight, held, sems, first):
    cols = weight.shape[1] // COLUMNS
    return [
        pltpu.make_async_copy(
            weight.at[:, j * cols : (j + 1) * cols], held.at[:, j * cols : (j + 1) * cols], sems.at[first + j]
        )
        for j in range(COLUMNS)
    ]


def make_source(hid, ray, source):
    both = hid[...].astype(F32) + ray[...].astype(F32)
    source[...] = both.astype(BF16).reshape(source.shape)


def place(blocks, first, base, feats, count, tok):
    for head in range(feats.shape[0] // HEAD_DIM):
        rows = slice(head * HEAD_DIM, (head + 1) * HEAD_DIM)
        for i in range(count):
            at = (base + i) * HEAD_DIM
            blocks[first + head, at : at + HEAD_DIM, :] = feats[rows, i * tok : (i + 1) * tok]


def pack_queries_kernel(
    view, hidden, rays, weight, obs_k, obs_v, out, hid, ray, held, obs, source, blocks, in_sem, out_sem
):
    views, tok = hidden.shape[:2]
    inputs = [pltpu.make_async_copy(hidden, hid, in_sem.at[0]), pltpu.make_async_copy(rays, ray, in_sem.at[1])]
    observed = [pltpu.make_async_copy(o, obs, in_sem.at[2]) for o in (obs_k, obs_v)]
    columns = column_loads(weight, held, in_sem, 3)
    for kind in range(2):

        @pl.when(view[0] == kind)
        def _():
            observed[kind].start()

    for c in inputs + columns:
        c.start()
    base = views * HEAD_DIM
    sends = []

    def send(place_of):
        sends.append(pltpu.make_async_copy(blocks.at[place_of], out.at[place_of], out_sem.at[len(sends)]))
        sends[-1].start()

    observed[0].wait()
    place(blocks, 0, views, obs[...].reshape(-1, obs.shape[-1]).T, obs.shape[0], tok)
    send((slice(None), slice(base, None)))
    for c in inputs:
        c.wait()
    make_source(hid, ray, source)
    cols = weight.shape[1] // COLUMNS
    heads = HEADS // COLUMNS
    for j in range(COLUMNS):
        columns[j].wait()
        feats = dot(source[...], held[:, j * cols : (j + 1) * cols]).astype(BF16) * jnp.asarray(HEAD_DIM**-0.5, BF16)
        place(blocks, j * heads, 0, feats.T, views, tok)
        send((slice(j * heads, (j + 1) * heads), slice(0, base)))
    for c in sends:
        c.wait()


def pack_queries(view, hidden, rays, weight, obs_k, obs_v):
    views, tok, width = hidden.shape
    shape = (HEADS, (views + obs_k.shape[0]) * HEAD_DIM, tok)
    return pl.pallas_call(
        pack_queries_kernel,
        in_specs=[pl.BlockSpec(memory_space=pltpu.SMEM)] + [HBM] * 5,
        out_specs=HBM,
        out_shape=jax.ShapeDtypeStruct(shape, BF16),
        scratch_shapes=[
            pltpu.VMEM(hidden.shape, BF16),
            pltpu.VMEM(rays.shape, BF16),
            pltpu.VMEM(weight.shape, BF16),
            pltpu.VMEM(obs_k.shape, BF16),
            pltpu.VMEM((views * tok, width), BF16),
            pltpu.VMEM(shape, BF16),
            pltpu.SemaphoreType.DMA((3 + COLUMNS,)),
            pltpu.SemaphoreType.DMA((1 + COLUMNS,)),
        ],
        compiler_params=params(58),
        cost_estimate=cost(2 * views * tok * width * width, 6 * MIB),
        name="pack_queries",
    )(view, hidden, rays, weight, obs_k, obs_v)


def pack_pairs_kernel(
    view, hidden, rays, w_key, w_value, keep, give, hid, ray, held_k, held_v, source, blocks, in_sem, out_sem
):
    views, tok = hidden.shape[:2]
    inputs = [pltpu.make_async_copy(hidden, hid, in_sem.at[0]), pltpu.make_async_copy(rays, ray, in_sem.at[1])]
    columns = column_loads(w_key, held_k, in_sem, 2) + column_loads(w_value, held_v, in_sem, 2 + COLUMNS)
    for c in inputs + columns:
        c.start()
    for c in inputs:
        c.wait()
    make_source(hid, ray, source)
    cols = w_key.shape[1] // COLUMNS
    heads = HEADS // COLUMNS
    for i, held in enumerate((held_k, held_v)):
        for j in range(COLUMNS):
            columns[i * COLUMNS + j].wait()
            feats = dot(source[...], held[:, j * cols : (j + 1) * cols]).astype(BF16)
            place(blocks, j * heads, i * views, feats.T, views, tok)
    half = keep.shape[0]
    sends = [
        pltpu.make_async_copy(blocks.at[pl.ds(side * half, half)], out, out_sem.at[i])
        for i, (side, out) in enumerate(((view[0], keep), (1 - view[0], give)))
    ]
    for c in sends:
        c.start()
    for c in sends:
        c.wait()


def pack_pairs(view, hidden, rays, w_key, w_value):
    views, tok, width = hidden.shape
    shape = (HEADS, 2 * views * HEAD_DIM, tok)
    return pl.pallas_call(
        pack_pairs_kernel,
        in_specs=[pl.BlockSpec(memory_space=pltpu.SMEM)] + [HBM] * 4,
        out_specs=[HBM, HBM],
        out_shape=[jax.ShapeDtypeStruct((HEADS // 2,) + shape[1:], BF16)] * 2,
        scratch_shapes=[
            pltpu.VMEM(hidden.shape, BF16),
            pltpu.VMEM(rays.shape, BF16),
            pltpu.VMEM(w_key.shape, BF16),
            pltpu.VMEM(w_value.shape, BF16),
            pltpu.VMEM((views * tok, width), BF16),
            pltpu.VMEM(shape, BF16),
            pltpu.SemaphoreType.DMA((2 + 2 * COLUMNS,)),
            pltpu.SemaphoreType.DMA((2,)),
        ],
        compiler_params=params(58),
        cost_estimate=cost(4 * views * tok * width * width, 7 * MIB),
        name="pack_pairs",
    )(view, hidden, rays, w_key, w_value)


def ones_rows(count, ones, lanes):
    row = lax.broadcasted_iota(jnp.int32, (count, lanes), 0)
    return jnp.where(row < ones, 1.0, 0.0).astype(BF16)


def store_keys(keys, at, turned):
    tok = turned.shape[1]
    full = jnp.concatenate([turned, ones_rows(KEY_COLS - HEAD_DIM, 3, tok)], axis=0)
    keys[at : at + tok, :] = full.T


def offset_rows(top):
    first = top.astype(BF16)
    rest = top - first.astype(F32)
    second = rest.astype(BF16)
    third = rest - second.astype(F32)
    row = lax.broadcasted_iota(jnp.int32, (KEY_COLS - HEAD_DIM, top.shape[1]), 0)
    picked = jnp.where(row == 0, first.astype(F32), 0.0)
    picked = jnp.where(row == 1, second.astype(F32), picked)
    picked = jnp.where(row == 2, third, picked)
    return (-picked).astype(BF16)


def block_max(keys, at, count, block, query, top):
    def step(i, top):
        start = pl.multiple_of(at + i * block, block)
        scores = dot(keys[pl.ds(start, block), :], query)
        return jnp.maximum(top, jnp.max(scores, axis=0, keepdims=True))

    return lax.fori_loop(0, count // block, step, top)


def weighted(keys, values, start, count, query):
    weights = jnp.exp(dot(keys[pl.ds(start, count), :], query)).astype(BF16)
    return dot(values[:, pl.ds(start, count)], weights)


def observed_kernel(packed, query_out, sums_out, keys, values, sums, sems):
    patches = packed.shape[0] // 2
    tok = packed.shape[2]
    views = query_out.shape[0]
    here = views // 2
    obs = packed.shape[1] // HEAD_DIM - here
    span = patches * tok
    for o in range(obs):
        rows = slice((here + o) * HEAD_DIM, (here + o + 1) * HEAD_DIM)
        for p in range(patches):
            at = (o * patches + p) * tok
            store_keys(keys, at, packed[p, rows, :])
            values[0:HEAD_DIM, at : at + tok] = packed[patches + p, rows, :]
    values[HEAD_DIM:, :] = jnp.ones((VALUE_ROWS - HEAD_DIM, obs * span), BF16)
    for u in range(views):
        rows = slice((u % here) * HEAD_DIM, (u % here + 1) * HEAD_DIM)
        query = jnp.concatenate([packed[(u // here) * patches + p, rows, :] for p in range(patches)], axis=1)
        query_out[u, 0:HEAD_DIM, :] = query
        top = jnp.max(dot(keys[0:tok, 0:HEAD_DIM], query), axis=0, keepdims=True)
        query_out[u, HEAD_DIM:, :] = offset_rows(top)

    def one_view(u, block):
        query = query_out[u]
        total = None
        for o in range(obs * span // block):
            term = weighted(keys, values, o * block, block, query)
            total = term if total is None else total + term
        sums[u] = total

    def send(u):
        return pltpu.make_async_copy(sums.at[u], sums_out.at[u], sems.at[u])

    @pl.loop(0, views)
    def _(u):
        one_view(u, span)
        send(u).start()

    largest = jnp.max(sums[:, SUM_ROW : SUM_ROW + 1, :])
    for u in range(views):
        send(u).wait()

    @pl.when(jnp.logical_not(largest < LIMIT))
    def _():
        @pl.loop(0, views)
        def _(u):
            query_out[u, HEAD_DIM:, :] = jnp.zeros((KEY_COLS - HEAD_DIM, span), BF16)
            low = jnp.full((1, span), -jnp.inf, F32)
            top = block_max(keys, 0, obs * span, tok, query_out[u], low)
            query_out[u, HEAD_DIM:, :] = offset_rows(top)
            sums[u] = jnp.zeros(sums.shape[1:], F32)

            @pl.loop(0, obs * patches)
            def _(i):
                sums[u] += weighted(keys, values, pl.multiple_of(i * tok, tok), tok, query_out[u])

            send(u).start()
            send(u).wait()


def observed_part(packed, views, obs):
    sources, rows, tok = packed.shape
    span = sources // 2 * tok
    vmem = pl.BlockSpec(memory_space=pltpu.VMEM)
    return pl.pallas_call(
        observed_kernel,
        in_specs=[vmem],
        out_specs=[vmem, pl.BlockSpec(memory_space=pltpu.MemorySpace.HBM)],
        out_shape=[
            jax.ShapeDtypeStruct((views, KEY_COLS, span), BF16),
            pltpu.MemorySpace.HBM((views, VALUE_ROWS, span), F32),
        ],
        scratch_shapes=[
            pltpu.VMEM((obs * span, KEY_COLS), BF16),
            pltpu.VMEM((VALUE_ROWS, obs * span), BF16),
            pltpu.VMEM((views, VALUE_ROWS, span), F32),
            pltpu.SemaphoreType.DMA((views,)),
        ],
        compiler_params=params(32),
        cost_estimate=cost(8 * views * obs * span * span * HEAD_DIM, 4 * MIB),
        name="observed_part",
    )(packed)


def generated_kernel(view_set, view, query, before, packed, out, keys, values, sums, pairs, early, sem):
    patches = packed.shape[0]
    tok = packed.shape[2]
    views = query.shape[0]
    here = views // 2
    span = patches * tok
    fetch = pltpu.make_async_copy(before, early, sem)
    fetch.start()

    def key_set(w):
        return view_set[jnp.bitwise_xor(w, here * view[0])]

    count = jnp.int32(0)
    for u in range(views):
        for w in range(views):
            pairs[count] = u * views + w
            count = count + (view_set[u] == key_set(w)).astype(jnp.int32)
    for w in range(views):
        base = (w // here * 2 * here + w % here) * HEAD_DIM
        for p in range(patches):
            at = (w * patches + p) * tok
            store_keys(keys, at, packed[p, base : base + HEAD_DIM, :])
            value_base = base + here * HEAD_DIM
            values[0:HEAD_DIM, at : at + tok] = packed[p, value_base : value_base + HEAD_DIM, :]
    values[HEAD_DIM:, :] = jnp.ones((VALUE_ROWS - HEAD_DIM, views * span), BF16)
    sums[...] = jnp.zeros(sums.shape, F32)

    def one_pair(i):
        u = pairs[i] // views
        start = pl.multiple_of((pairs[i] % views) * span, span)
        return u, weighted(keys, values, start, span, query[u])

    @pl.loop(0, count // 2)
    def _(i):
        u0, term0 = one_pair(2 * i)
        u1, term1 = one_pair(2 * i + 1)
        sums[u0] += term0
        sums[u1] += term1

    largest = jnp.max(sums[:, SUM_ROW : SUM_ROW + 1, :])
    fetch.wait()

    @pl.when(jnp.logical_not(largest < LIMIT))
    def _():
        @pl.loop(0, views)
        def _(u):
            rows = -query[u, HEAD_DIM : HEAD_DIM + 16, :].astype(F32)
            old = rows[0:1] + rows[1:2] + rows[2:3]
            plain = jnp.concatenate(
                [query[u, 0:HEAD_DIM, :], jnp.zeros((KEY_COLS - HEAD_DIM, span), BF16)], axis=0
            )

            def look(w, top):
                seen = jnp.where(view_set[u] == key_set(w), span, 0)
                return block_max(keys, w * span, seen, tok, plain, top)

            top = lax.fori_loop(0, views, look, old)
            shifted = jnp.concatenate([query[u, 0:HEAD_DIM, :], offset_rows(top)], axis=0)
            early[u] = early[u] * jnp.exp(old - top)
            sums[u] = jnp.zeros(sums.shape[1:], F32)

            @pl.loop(0, views)
            def _(w):
                @pl.when(view_set[u] == key_set(w))
                def _():
                    @pl.loop(0, patches)
                    def _(p):
                        start = pl.multiple_of(w * span + p * tok, tok)
                        sums[u] += weighted(keys, values, start, tok, shifted)

    for u in range(views):
        total = sums[u] + early[u]
        context = (total[0:HEAD_DIM] / total[SUM_ROW : SUM_ROW + 1]).astype(BF16)
        rows = slice((u % here) * HEAD_DIM, (u % here + 1) * HEAD_DIM)
        for p in range(patches):
            out[(u // here) * patches + p, rows, :] = context[:, p * tok : (p + 1) * tok]


def generated_part(view_set, view, query, before, packed):
    patches, rows, tok = packed.shape
    views, _, span = query.shape
    vmem = pl.BlockSpec(memory_space=pltpu.VMEM)
    return pl.pallas_call(
        generated_kernel,
        in_specs=[
            pl.BlockSpec(memory_space=pltpu.SMEM),
            pl.BlockSpec(memory_space=pltpu.SMEM),
            vmem,
            pl.BlockSpec(memory_space=pltpu.MemorySpace.HBM),
            vmem,
        ],
        out_specs=vmem,
        out_shape=jax.ShapeDtypeStruct((2 * patches, rows // 4, tok), BF16),
        scratch_shapes=[
            pltpu.VMEM((views * span, KEY_COLS), BF16),
            pltpu.VMEM((VALUE_ROWS, views * span), BF16),
            pltpu.VMEM((views, VALUE_ROWS, span), F32),
            pltpu.SMEM((views * views + 1,), jnp.int32),
            pltpu.VMEM((views, VALUE_ROWS, span), F32),
            pltpu.SemaphoreType.DMA,
        ],
        compiler_params=params(32),
        cost_estimate=cost(6 * views * views * span * span * HEAD_DIM, 4 * MIB),
        name="generated_part",
    )(view_set, view, query, pltpu.with_memory_space_constraint(before, pltpu.MemorySpace.HBM), packed)


def project_out_kernel(packed, weight, out, context, blocks, sems):
    views, tok = out.shape[:2]
    for i in range(views):
        rows = packed[:, i * HEAD_DIM : (i + 1) * HEAD_DIM, :].reshape(HEADS * HEAD_DIM, tok)
        context[i * tok : (i + 1) * tok, :] = rows.T
    copies = []
    cols = weight.shape[1] // 2
    for j in range(2):
        at = slice(j * cols, (j + 1) * cols)
        blocks[:, :, at] = dot(context[...], weight[:, at]).astype(BF16).reshape(views, tok, cols)
        copies.append(pltpu.make_async_copy(blocks.at[:, :, at], out.at[:, :, at], sems.at[j]))
        copies[j].start()
    for c in copies:
        c.wait()


def project_out(packed, weight):
    heads, rows, tok = packed.shape
    views = rows // HEAD_DIM
    width = weight.shape[0]
    vmem = pl.BlockSpec(memory_space=pltpu.VMEM)
    return pl.pallas_call(
        project_out_kernel,
        in_specs=[vmem, vmem],
        out_specs=pl.BlockSpec(memory_space=pltpu.MemorySpace.HBM),
        out_shape=jax.ShapeDtypeStruct((views, tok, width), BF16),
        scratch_shapes=[
            pltpu.VMEM((views * tok, width), BF16),
            pltpu.VMEM((views, tok, width), BF16),
            pltpu.SemaphoreType.DMA((2,)),
        ],
        compiler_params=params(24),
        cost_estimate=cost(2 * views * tok * width * width, 4 * MIB),
        name="project_out",
    )(packed, weight)


def exchange(blocks):
    return lax.all_to_all(blocks, ("view", "patch"), split_axis=0, concat_axis=0, tiled=True)


def on_device(hidden, rays, view_set, obs_keys, obs_values, w_query, w_key, w_value, w_out):
    views = view_set.shape[0]
    view = lax.axis_index("view").astype(jnp.int32).reshape(1)
    queries = exchange(pack_queries(view, hidden, rays, w_query, obs_keys, obs_values))
    keep, give = pack_pairs(view, hidden, rays, w_key, w_value)
    got = lax.ppermute(give, "view", [(0, 1), (1, 0)])
    pairs = jnp.concatenate([keep, got], axis=1)
    pairs = lax.all_to_all(pairs, "patch", split_axis=0, concat_axis=0, tiled=True)
    query, before = observed_part(queries, views, obs_keys.shape[0])
    context = exchange(generated_part(view_set, view, query, before, pairs))
    return project_out(context, w_out)


def solution(mesh):
    return jax.shard_map(
        on_device,
        mesh=mesh,
        in_specs=(
            P(("group", "view"), "patch", None),
            P(("group", "view"), "patch", None),
            P("group"),
            P(None, "patch", None),
            P(None, "patch", None),
            P(),
            P(),
            P(),
            P(),
        ),
        out_specs=P(("group", "view"), "patch", None),
        check_vma=False,
    )
```

```python
import jax
import jax.numpy as jnp
from jax import lax
from jax.experimental import pallas as pl
from jax.experimental.pallas import tpu as pltpu
from jax.sharding import PartitionSpec as P

HEADS = 16
HEAD_DIM = 64
SUM_ROW = HEAD_DIM
VALUE_ROWS = HEAD_DIM + 16
KEY_COLS = 2 * HEAD_DIM
LIMIT = 2.0**100
BF16 = jnp.bfloat16
F32 = jnp.float32
MIB = 2**20


def dot(a, b):
    return jnp.dot(a, b, preferred_element_type=F32)


def params(mib):
    return pltpu.CompilerParams(vmem_limit_bytes=mib * MIB)


def cost(flops, nbytes):
    return pl.CostEstimate(flops=int(flops), bytes_accessed=int(nbytes), transcendentals=0)


HBM = pl.BlockSpec(memory_space=pltpu.MemorySpace.HBM)
COLUMNS = 2


def column_loads(weight, held, sems, first):
    cols = weight.shape[1] // COLUMNS
    return [
        pltpu.make_async_copy(
            weight.at[:, j * cols : (j + 1) * cols], held.at[:, j * cols : (j + 1) * cols], sems.at[first + j]
        )
        for j in range(COLUMNS)
    ]


def make_source(hid, ray, source):
    both = hid[...].astype(F32) + ray[...].astype(F32)
    source[...] = both.astype(BF16).reshape(source.shape)


def place(blocks, first, base, feats, count, tok):
    for head in range(feats.shape[0] // HEAD_DIM):
        rows = slice(head * HEAD_DIM, (head + 1) * HEAD_DIM)
        for i in range(count):
            at = (base + i) * HEAD_DIM
            blocks[first + head, at : at + HEAD_DIM, :] = feats[rows, i * tok : (i + 1) * tok]


def pack_queries_kernel(
    view, hidden, rays, weight, obs_k, obs_v, out, hid, ray, held, obs, source, blocks, in_sem, out_sem
):
    views, tok = hidden.shape[:2]
    inputs = [pltpu.make_async_copy(hidden, hid, in_sem.at[0]), pltpu.make_async_copy(rays, ray, in_sem.at[1])]
    observed = [pltpu.make_async_copy(o, obs, in_sem.at[2]) for o in (obs_k, obs_v)]
    columns = column_loads(weight, held, in_sem, 3)
    for kind in range(2):

        @pl.when(view[0] == kind)
        def _():
            observed[kind].start()

    for c in inputs + columns:
        c.start()
    base = views * HEAD_DIM
    sends = []

    def send(place_of):
        sends.append(pltpu.make_async_copy(blocks.at[place_of], out.at[place_of], out_sem.at[len(sends)]))
        sends[-1].start()

    observed[0].wait()
    place(blocks, 0, views, obs[...].reshape(-1, obs.shape[-1]).T, obs.shape[0], tok)
    send((slice(None), slice(base, None)))
    for c in inputs:
        c.wait()
    make_source(hid, ray, source)
    cols = weight.shape[1] // COLUMNS
    heads = HEADS // COLUMNS
    for j in range(COLUMNS):
        columns[j].wait()
        feats = dot(source[...], held[:, j * cols : (j + 1) * cols]).astype(BF16) * jnp.asarray(HEAD_DIM**-0.5, BF16)
        place(blocks, j * heads, 0, feats.T, views, tok)
        send((slice(j * heads, (j + 1) * heads), slice(0, base)))
    for c in sends:
        c.wait()


def pack_queries(view, hidden, rays, weight, obs_k, obs_v):
    views, tok, width = hidden.shape
    shape = (HEADS, (views + obs_k.shape[0]) * HEAD_DIM, tok)
    return pl.pallas_call(
        pack_queries_kernel,
        in_specs=[pl.BlockSpec(memory_space=pltpu.SMEM)] + [HBM] * 5,
        out_specs=HBM,
        out_shape=jax.ShapeDtypeStruct(shape, BF16),
        scratch_shapes=[
            pltpu.VMEM(hidden.shape, BF16),
            pltpu.VMEM(rays.shape, BF16),
            pltpu.VMEM(weight.shape, BF16),
            pltpu.VMEM(obs_k.shape, BF16),
            pltpu.VMEM((views * tok, width), BF16),
            pltpu.VMEM(shape, BF16),
            pltpu.SemaphoreType.DMA((3 + COLUMNS,)),
            pltpu.SemaphoreType.DMA((1 + COLUMNS,)),
        ],
        compiler_params=params(58),
        cost_estimate=cost(2 * views * tok * width * width, 6 * MIB),
        name="pack_queries",
    )(view, hidden, rays, weight, obs_k, obs_v)


def pack_pairs_kernel(
    view, hidden, rays, w_key, w_value, keep, give, hid, ray, held_k, held_v, source, blocks, in_sem, out_sem
):
    views, tok = hidden.shape[:2]
    inputs = [pltpu.make_async_copy(hidden, hid, in_sem.at[0]), pltpu.make_async_copy(rays, ray, in_sem.at[1])]
    columns = column_loads(w_key, held_k, in_sem, 2) + column_loads(w_value, held_v, in_sem, 2 + COLUMNS)
    for c in inputs + columns:
        c.start()
    for c in inputs:
        c.wait()
    make_source(hid, ray, source)
    cols = w_key.shape[1] // COLUMNS
    heads = HEADS // COLUMNS
    for i, held in enumerate((held_k, held_v)):
        for j in range(COLUMNS):
            columns[i * COLUMNS + j].wait()
            feats = dot(source[...], held[:, j * cols : (j + 1) * cols]).astype(BF16)
            place(blocks, j * heads, i * views, feats.T, views, tok)
    half = keep.shape[0]
    sends = [
        pltpu.make_async_copy(blocks.at[pl.ds(side * half, half)], out, out_sem.at[i])
        for i, (side, out) in enumerate(((view[0], keep), (1 - view[0], give)))
    ]
    for c in sends:
        c.start()
    for c in sends:
        c.wait()


def pack_pairs(view, hidden, rays, w_key, w_value):
    views, tok, width = hidden.shape
    shape = (HEADS, 2 * views * HEAD_DIM, tok)
    return pl.pallas_call(
        pack_pairs_kernel,
        in_specs=[pl.BlockSpec(memory_space=pltpu.SMEM)] + [HBM] * 4,
        out_specs=[HBM, HBM],
        out_shape=[jax.ShapeDtypeStruct((HEADS // 2,) + shape[1:], BF16)] * 2,
        scratch_shapes=[
            pltpu.VMEM(hidden.shape, BF16),
            pltpu.VMEM(rays.shape, BF16),
            pltpu.VMEM(w_key.shape, BF16),
            pltpu.VMEM(w_value.shape, BF16),
            pltpu.VMEM((views * tok, width), BF16),
            pltpu.VMEM(shape, BF16),
            pltpu.SemaphoreType.DMA((2 + 2 * COLUMNS,)),
            pltpu.SemaphoreType.DMA((2,)),
        ],
        compiler_params=params(58),
        cost_estimate=cost(4 * views * tok * width * width, 7 * MIB),
        name="pack_pairs",
    )(view, hidden, rays, w_key, w_value)


def ones_rows(count, ones, lanes):
    row = lax.broadcasted_iota(jnp.int32, (count, lanes), 0)
    return jnp.where(row < ones, 1.0, 0.0).astype(BF16)


def store_keys(keys, at, turned):
    tok = turned.shape[1]
    full = jnp.concatenate([turned, ones_rows(KEY_COLS - HEAD_DIM, 3, tok)], axis=0)
    keys[at : at + tok, :] = full.T


def offset_rows(top):
    first = top.astype(BF16)
    rest = top - first.astype(F32)
    second = rest.astype(BF16)
    third = rest - second.astype(F32)
    row = lax.broadcasted_iota(jnp.int32, (KEY_COLS - HEAD_DIM, top.shape[1]), 0)
    picked = jnp.where(row == 0, first.astype(F32), 0.0)
    picked = jnp.where(row == 1, second.astype(F32), picked)
    picked = jnp.where(row == 2, third, picked)
    return (-picked).astype(BF16)


def block_max(keys, at, count, block, query, top):
    def step(i, top):
        start = pl.multiple_of(at + i * block, block)
        scores = dot(keys[pl.ds(start, block), :], query)
        return jnp.maximum(top, jnp.max(scores, axis=0, keepdims=True))

    return lax.fori_loop(0, count // block, step, top)


def weighted(keys, values, start, count, query):
    weights = jnp.exp(dot(keys[pl.ds(start, count), :], query)).astype(BF16)
    return dot(values[:, pl.ds(start, count)], weights)


def observed_kernel(packed, query_out, sums_out, keys, values, sums, sems):
    patches = packed.shape[0] // 2
    tok = packed.shape[2]
    views = query_out.shape[0]
    here = views // 2
    obs = packed.shape[1] // HEAD_DIM - here
    span = patches * tok
    for o in range(obs):
        rows = slice((here + o) * HEAD_DIM, (here + o + 1) * HEAD_DIM)
        for p in range(patches):
            at = (o * patches + p) * tok
            store_keys(keys, at, packed[p, rows, :])
            values[0:HEAD_DIM, at : at + tok] = packed[patches + p, rows, :]
    values[HEAD_DIM:, :] = jnp.ones((VALUE_ROWS - HEAD_DIM, obs * span), BF16)
    for u in range(views):
        rows = slice((u % here) * HEAD_DIM, (u % here + 1) * HEAD_DIM)
        query = jnp.concatenate([packed[(u // here) * patches + p, rows, :] for p in range(patches)], axis=1)
        query_out[u, 0:HEAD_DIM, :] = query
        top = jnp.max(dot(keys[0:tok, 0:HEAD_DIM], query), axis=0, keepdims=True)
        query_out[u, HEAD_DIM:, :] = offset_rows(top)

    def one_view(u, block):
        query = query_out[u]
        total = None
        for o in range(obs * span // block):
            term = weighted(keys, values, o * block, block, query)
            total = term if total is None else total + term
        sums[u] = total

    def send(u):
        return pltpu.make_async_copy(sums.at[u], sums_out.at[u], sems.at[u])

    @pl.loop(0, views)
    def _(u):
        one_view(u, span)
        send(u).start()

    largest = jnp.max(sums[:, SUM_ROW : SUM_ROW + 1, :])
    for u in range(views):
        send(u).wait()

    @pl.when(jnp.logical_not(largest < LIMIT))
    def _():
        @pl.loop(0, views)
        def _(u):
            query_out[u, HEAD_DIM:, :] = jnp.zeros((KEY_COLS - HEAD_DIM, span), BF16)
            low = jnp.full((1, span), -jnp.inf, F32)
            top = block_max(keys, 0, obs * span, tok, query_out[u], low)
            query_out[u, HEAD_DIM:, :] = offset_rows(top)
            sums[u] = jnp.zeros(sums.shape[1:], F32)

            @pl.loop(0, obs * patches)
            def _(i):
                sums[u] += weighted(keys, values, pl.multiple_of(i * tok, tok), tok, query_out[u])

            send(u).start()
            send(u).wait()


def observed_part(packed, views, obs):
    sources, rows, tok = packed.shape
    span = sources // 2 * tok
    vmem = pl.BlockSpec(memory_space=pltpu.VMEM)
    return pl.pallas_call(
        observed_kernel,
        in_specs=[vmem],
        out_specs=[vmem, pl.BlockSpec(memory_space=pltpu.MemorySpace.HBM)],
        out_shape=[
            jax.ShapeDtypeStruct((views, KEY_COLS, span), BF16),
            pltpu.MemorySpace.HBM((views, VALUE_ROWS, span), F32),
        ],
        scratch_shapes=[
            pltpu.VMEM((obs * span, KEY_COLS), BF16),
            pltpu.VMEM((VALUE_ROWS, obs * span), BF16),
            pltpu.VMEM((views, VALUE_ROWS, span), F32),
            pltpu.SemaphoreType.DMA((views,)),
        ],
        compiler_params=params(32),
        cost_estimate=cost(8 * views * obs * span * span * HEAD_DIM, 4 * MIB),
        name="observed_part",
    )(packed)


def generated_kernel(view_set, view, query, before, packed, out, keys, values, sums, pairs, early, sem):
    patches = packed.shape[0]
    tok = packed.shape[2]
    views = query.shape[0]
    here = views // 2
    span = patches * tok
    fetch = pltpu.make_async_copy(before, early, sem)
    fetch.start()

    def key_set(w):
        return view_set[jnp.bitwise_xor(w, here * view[0])]

    count = jnp.int32(0)
    for u in range(views):
        for w in range(views):
            pairs[count] = u * views + w
            count = count + (view_set[u] == key_set(w)).astype(jnp.int32)
    for w in range(views):
        base = (w // here * 2 * here + w % here) * HEAD_DIM
        for p in range(patches):
            at = (w * patches + p) * tok
            store_keys(keys, at, packed[p, base : base + HEAD_DIM, :])
            value_base = base + here * HEAD_DIM
            values[0:HEAD_DIM, at : at + tok] = packed[p, value_base : value_base + HEAD_DIM, :]
    values[HEAD_DIM:, :] = jnp.ones((VALUE_ROWS - HEAD_DIM, views * span), BF16)
    sums[...] = jnp.zeros(sums.shape, F32)

    def one_pair(i):
        u = pairs[i] // views
        start = pl.multiple_of((pairs[i] % views) * span, span)
        return u, weighted(keys, values, start, span, query[u])

    def several(first, width):
        for u, term in [one_pair(first + i) for i in range(width)]:
            sums[u] += term

    @pl.when(count % 5 == 0)
    def _():
        @pl.loop(0, count // 5)
        def _(i):
            several(5 * i, 5)

    @pl.when(count % 5 != 0)
    def _():
        @pl.loop(0, count // 4)
        def _(i):
            several(4 * i, 4)

    largest = jnp.max(sums[:, SUM_ROW : SUM_ROW + 1, :])
    fetch.wait()

    @pl.when(jnp.logical_not(largest < LIMIT))
    def _():
        @pl.loop(0, views)
        def _(u):
            rows = -query[u, HEAD_DIM : HEAD_DIM + 16, :].astype(F32)
            old = rows[0:1] + rows[1:2] + rows[2:3]
            plain = jnp.concatenate(
                [query[u, 0:HEAD_DIM, :], jnp.zeros((KEY_COLS - HEAD_DIM, span), BF16)], axis=0
            )

            def look(w, top):
                seen = jnp.where(view_set[u] == key_set(w), span, 0)
                return block_max(keys, w * span, seen, tok, plain, top)

            top = lax.fori_loop(0, views, look, old)
            shifted = jnp.concatenate([query[u, 0:HEAD_DIM, :], offset_rows(top)], axis=0)
            early[u] = early[u] * jnp.exp(old - top)
            sums[u] = jnp.zeros(sums.shape[1:], F32)

            @pl.loop(0, views)
            def _(w):
                @pl.when(view_set[u] == key_set(w))
                def _():
                    @pl.loop(0, patches)
                    def _(p):
                        start = pl.multiple_of(w * span + p * tok, tok)
                        sums[u] += weighted(keys, values, start, tok, shifted)

    for u in range(views):
        total = sums[u] + early[u]
        context = (total[0:HEAD_DIM] * (1.0 / total[SUM_ROW : SUM_ROW + 1])).astype(BF16)
        rows = slice((u % here) * HEAD_DIM, (u % here + 1) * HEAD_DIM)
        for p in range(patches):
            out[(u // here) * patches + p, rows, :] = context[:, p * tok : (p + 1) * tok]


def generated_part(view_set, view, query, before, packed):
    patches, rows, tok = packed.shape
    views, _, span = query.shape
    vmem = pl.BlockSpec(memory_space=pltpu.VMEM)
    return pl.pallas_call(
        generated_kernel,
        in_specs=[
            pl.BlockSpec(memory_space=pltpu.SMEM),
            pl.BlockSpec(memory_space=pltpu.SMEM),
            vmem,
            pl.BlockSpec(memory_space=pltpu.MemorySpace.HBM),
            vmem,
        ],
        out_specs=vmem,
        out_shape=jax.ShapeDtypeStruct((2 * patches, rows // 4, tok), BF16),
        scratch_shapes=[
            pltpu.VMEM((views * span, KEY_COLS), BF16),
            pltpu.VMEM((VALUE_ROWS, views * span), BF16),
            pltpu.VMEM((views, VALUE_ROWS, span), F32),
            pltpu.SMEM((views * views + 1,), jnp.int32),
            pltpu.VMEM((views, VALUE_ROWS, span), F32),
            pltpu.SemaphoreType.DMA,
        ],
        compiler_params=params(32),
        cost_estimate=cost(6 * views * views * span * span * HEAD_DIM, 4 * MIB),
        name="generated_part",
    )(view_set, view, query, pltpu.with_memory_space_constraint(before, pltpu.MemorySpace.HBM), packed)


def project_out_kernel(packed, weight, out, context, blocks, sems):
    views, tok = out.shape[:2]
    for i in range(views):
        rows = packed[:, i * HEAD_DIM : (i + 1) * HEAD_DIM, :].reshape(HEADS * HEAD_DIM, tok)
        context[i * tok : (i + 1) * tok, :] = rows.T
    copies = []
    cols = weight.shape[1] // 2
    for j in range(2):
        at = slice(j * cols, (j + 1) * cols)
        blocks[:, :, at] = dot(context[...], weight[:, at]).astype(BF16).reshape(views, tok, cols)
        copies.append(pltpu.make_async_copy(blocks.at[:, :, at], out.at[:, :, at], sems.at[j]))
        copies[j].start()
    for c in copies:
        c.wait()


def project_out(packed, weight):
    heads, rows, tok = packed.shape
    views = rows // HEAD_DIM
    width = weight.shape[0]
    vmem = pl.BlockSpec(memory_space=pltpu.VMEM)
    return pl.pallas_call(
        project_out_kernel,
        in_specs=[vmem, vmem],
        out_specs=pl.BlockSpec(memory_space=pltpu.MemorySpace.HBM),
        out_shape=jax.ShapeDtypeStruct((views, tok, width), BF16),
        scratch_shapes=[
            pltpu.VMEM((views * tok, width), BF16),
            pltpu.VMEM((views, tok, width), BF16),
            pltpu.SemaphoreType.DMA((2,)),
        ],
        compiler_params=params(24),
        cost_estimate=cost(2 * views * tok * width * width, 4 * MIB),
        name="project_out",
    )(packed, weight)


def exchange(blocks):
    return lax.all_to_all(blocks, ("view", "patch"), split_axis=0, concat_axis=0, tiled=True)


def on_device(hidden, rays, view_set, obs_keys, obs_values, w_query, w_key, w_value, w_out):
    views = view_set.shape[0]
    view = lax.axis_index("view").astype(jnp.int32).reshape(1)
    queries = exchange(pack_queries(view, hidden, rays, w_query, obs_keys, obs_values))
    keep, give = pack_pairs(view, hidden, rays, w_key, w_value)
    got = lax.ppermute(give, "view", [(0, 1), (1, 0)])
    pairs = jnp.concatenate([keep, got], axis=1)
    pairs = lax.all_to_all(pairs, "patch", split_axis=0, concat_axis=0, tiled=True)
    query, before = observed_part(queries, views, obs_keys.shape[0])
    context = exchange(generated_part(view_set, view, query, before, pairs))
    return project_out(context, w_out)


def solution(mesh):
    return jax.shard_map(
        on_device,
        mesh=mesh,
        in_specs=(
            P(("group", "view"), "patch", None),
            P(("group", "view"), "patch", None),
            P("group"),
            P(None, "patch", None),
            P(None, "patch", None),
            P(),
            P(),
            P(),
            P(),
        ),
        out_specs=P(("group", "view"), "patch", None),
        check_vma=False,
    )
```

```python
import jax
import jax.numpy as jnp
from jax import lax
from jax.experimental import pallas as pl
from jax.experimental.pallas import tpu as pltpu
from jax.sharding import PartitionSpec as P

HEADS = 16
HEAD_DIM = 64
SUM_ROW = HEAD_DIM
VALUE_ROWS = HEAD_DIM + 16
KEY_COLS = 2 * HEAD_DIM
LIMIT = 2.0**100
BF16 = jnp.bfloat16
F32 = jnp.float32
MIB = 2**20


def dot(a, b):
    return jnp.dot(a, b, preferred_element_type=F32)


def params(mib):
    return pltpu.CompilerParams(vmem_limit_bytes=mib * MIB)


def cost(flops, nbytes):
    return pl.CostEstimate(flops=int(flops), bytes_accessed=int(nbytes), transcendentals=0)


HBM = pl.BlockSpec(memory_space=pltpu.MemorySpace.HBM)
PATCHES = (0, 3, 2, 5, 4, 7, 6, 1)
COLUMNS = 2


def column_loads(weight, held, sems, first):
    cols = weight.shape[1] // COLUMNS
    return [
        pltpu.make_async_copy(
            weight.at[:, j * cols : (j + 1) * cols], held.at[:, j * cols : (j + 1) * cols], sems.at[first + j]
        )
        for j in range(COLUMNS)
    ]


def make_source(hid, ray, source):
    both = hid[...].astype(F32) + ray[...].astype(F32)
    source[...] = both.astype(BF16).reshape(source.shape)


def place(blocks, first, base, feats, count, tok, order=None):
    for head in range(feats.shape[0] // HEAD_DIM):
        to = first + head
        if order:
            to = to // len(order) * len(order) + order.index(to % len(order))
        rows = slice(head * HEAD_DIM, (head + 1) * HEAD_DIM)
        for i in range(count):
            at = (base + i) * HEAD_DIM
            blocks[to, at : at + HEAD_DIM, :] = feats[rows, i * tok : (i + 1) * tok]


def pack_queries_kernel(
    view, hidden, rays, weight, obs_k, obs_v, out, hid, ray, held, obs, source, blocks, in_sem, out_sem
):
    views, tok = hidden.shape[:2]
    inputs = [pltpu.make_async_copy(hidden, hid, in_sem.at[0]), pltpu.make_async_copy(rays, ray, in_sem.at[1])]
    observed = [pltpu.make_async_copy(o, obs, in_sem.at[2]) for o in (obs_k, obs_v)]
    columns = column_loads(weight, held, in_sem, 3)
    for kind in range(2):

        @pl.when(view[0] == kind)
        def _():
            observed[kind].start()

    for c in inputs + columns:
        c.start()
    base = views * HEAD_DIM
    sends = []

    def send(place_of):
        sends.append(pltpu.make_async_copy(blocks.at[place_of], out.at[place_of], out_sem.at[len(sends)]))
        sends[-1].start()

    observed[0].wait()
    place(blocks, 0, views, obs[...].reshape(-1, obs.shape[-1]).T, obs.shape[0], tok)
    send((slice(None), slice(base, None)))
    for c in inputs:
        c.wait()
    make_source(hid, ray, source)
    cols = weight.shape[1] // COLUMNS
    heads = HEADS // COLUMNS
    for j in range(COLUMNS):
        columns[j].wait()
        feats = dot(source[...], held[:, j * cols : (j + 1) * cols]).astype(BF16) * jnp.asarray(HEAD_DIM**-0.5, BF16)
        place(blocks, j * heads, 0, feats.T, views, tok)
        send((slice(j * heads, (j + 1) * heads), slice(0, base)))
    for c in sends:
        c.wait()


def pack_queries(view, hidden, rays, weight, obs_k, obs_v):
    views, tok, width = hidden.shape
    shape = (HEADS, (views + obs_k.shape[0]) * HEAD_DIM, tok)
    return pl.pallas_call(
        pack_queries_kernel,
        in_specs=[pl.BlockSpec(memory_space=pltpu.SMEM)] + [HBM] * 5,
        out_specs=HBM,
        out_shape=jax.ShapeDtypeStruct(shape, BF16),
        scratch_shapes=[
            pltpu.VMEM(hidden.shape, BF16),
            pltpu.VMEM(rays.shape, BF16),
            pltpu.VMEM(weight.shape, BF16),
            pltpu.VMEM(obs_k.shape, BF16),
            pltpu.VMEM((views * tok, width), BF16),
            pltpu.VMEM(shape, BF16),
            pltpu.SemaphoreType.DMA((3 + COLUMNS,)),
            pltpu.SemaphoreType.DMA((1 + COLUMNS,)),
        ],
        compiler_params=params(58),
        cost_estimate=cost(2 * views * tok * width * width, 6 * MIB),
        name="pack_queries",
    )(view, hidden, rays, weight, obs_k, obs_v)


def pack_pairs_kernel(
    view, hidden, rays, w_key, w_value, keep, give, hid, ray, held_k, held_v, source, blocks, in_sem, out_sem
):
    views, tok = hidden.shape[:2]
    inputs = [pltpu.make_async_copy(hidden, hid, in_sem.at[0]), pltpu.make_async_copy(rays, ray, in_sem.at[1])]
    columns = column_loads(w_key, held_k, in_sem, 2) + column_loads(w_value, held_v, in_sem, 2 + COLUMNS)
    for c in inputs + columns:
        c.start()
    for c in inputs:
        c.wait()
    make_source(hid, ray, source)
    cols = w_key.shape[1] // COLUMNS
    heads = HEADS // COLUMNS
    for i, held in enumerate((held_k, held_v)):
        for j in range(COLUMNS):
            columns[i * COLUMNS + j].wait()
            feats = dot(source[...], held[:, j * cols : (j + 1) * cols]).astype(BF16)
            place(blocks, j * heads, i * views, feats.T, views, tok, PATCHES)
    half = keep.shape[0]
    sends = [
        pltpu.make_async_copy(blocks.at[pl.ds(side * half, half)], out, out_sem.at[i])
        for i, (side, out) in enumerate(((view[0], keep), (1 - view[0], give)))
    ]
    for c in sends:
        c.start()
    for c in sends:
        c.wait()


def pack_pairs(view, hidden, rays, w_key, w_value):
    views, tok, width = hidden.shape
    shape = (HEADS, 2 * views * HEAD_DIM, tok)
    return pl.pallas_call(
        pack_pairs_kernel,
        in_specs=[pl.BlockSpec(memory_space=pltpu.SMEM)] + [HBM] * 4,
        out_specs=[HBM, HBM],
        out_shape=[jax.ShapeDtypeStruct((HEADS // 2,) + shape[1:], BF16)] * 2,
        scratch_shapes=[
            pltpu.VMEM(hidden.shape, BF16),
            pltpu.VMEM(rays.shape, BF16),
            pltpu.VMEM(w_key.shape, BF16),
            pltpu.VMEM(w_value.shape, BF16),
            pltpu.VMEM((views * tok, width), BF16),
            pltpu.VMEM(shape, BF16),
            pltpu.SemaphoreType.DMA((2 + 2 * COLUMNS,)),
            pltpu.SemaphoreType.DMA((2,)),
        ],
        compiler_params=params(58),
        cost_estimate=cost(4 * views * tok * width * width, 7 * MIB),
        name="pack_pairs",
    )(view, hidden, rays, w_key, w_value)


def ones_rows(count, ones, lanes):
    row = lax.broadcasted_iota(jnp.int32, (count, lanes), 0)
    return jnp.where(row < ones, 1.0, 0.0).astype(BF16)


def store_keys(keys, at, turned):
    tok = turned.shape[1]
    full = jnp.concatenate([turned, ones_rows(KEY_COLS - HEAD_DIM, 3, tok)], axis=0)
    keys[at : at + tok, :] = full.T


def offset_rows(top):
    first = top.astype(BF16)
    rest = top - first.astype(F32)
    second = rest.astype(BF16)
    third = rest - second.astype(F32)
    row = lax.broadcasted_iota(jnp.int32, (KEY_COLS - HEAD_DIM, top.shape[1]), 0)
    picked = jnp.where(row == 0, first.astype(F32), 0.0)
    picked = jnp.where(row == 1, second.astype(F32), picked)
    picked = jnp.where(row == 2, third, picked)
    return (-picked).astype(BF16)


def block_max(keys, at, count, block, query, top):
    def step(i, top):
        start = pl.multiple_of(at + i * block, block)
        scores = dot(keys[pl.ds(start, block), :], query)
        return jnp.maximum(top, jnp.max(scores, axis=0, keepdims=True))

    return lax.fori_loop(0, count // block, step, top)


def weighted(keys, values, start, count, query):
    weights = jnp.exp(dot(keys[pl.ds(start, count), :], query)).astype(BF16)
    return dot(values[:, pl.ds(start, count)], weights)


def observed_kernel(packed, query_out, sums_out, keys, values, sums, sems):
    patches = packed.shape[0] // 2
    tok = packed.shape[2]
    views = query_out.shape[0]
    here = views // 2
    obs = packed.shape[1] // HEAD_DIM - here
    span = patches * tok
    for o in range(obs):
        rows = slice((here + o) * HEAD_DIM, (here + o + 1) * HEAD_DIM)
        for p in range(patches):
            at = (o * patches + p) * tok
            store_keys(keys, at, packed[p, rows, :])
            values[0:HEAD_DIM, at : at + tok] = packed[patches + p, rows, :]
    values[HEAD_DIM:, :] = jnp.ones((VALUE_ROWS - HEAD_DIM, obs * span), BF16)
    for u in range(views):
        rows = slice((u % here) * HEAD_DIM, (u % here + 1) * HEAD_DIM)
        query = jnp.concatenate([packed[(u // here) * patches + p, rows, :] for p in range(patches)], axis=1)
        query_out[u, 0:HEAD_DIM, :] = query
        top = jnp.max(dot(keys[0:tok, 0:HEAD_DIM], query), axis=0, keepdims=True)
        query_out[u, HEAD_DIM:, :] = offset_rows(top)

    def one_view(u, block):
        query = query_out[u]
        total = None
        for o in range(obs * span // block):
            term = weighted(keys, values, o * block, block, query)
            total = term if total is None else total + term
        sums[u] = total

    def send(u):
        return pltpu.make_async_copy(sums.at[u], sums_out.at[u], sems.at[u])

    @pl.loop(0, views // 2)
    def _(i):
        for u in (2 * i, 2 * i + 1):
            one_view(u, span)
            send(u).start()

    largest = jnp.max(sums[:, SUM_ROW : SUM_ROW + 1, :])
    for u in range(views):
        send(u).wait()

    @pl.when(jnp.logical_not(largest < LIMIT))
    def _():
        @pl.loop(0, views)
        def _(u):
            query_out[u, HEAD_DIM:, :] = jnp.zeros((KEY_COLS - HEAD_DIM, span), BF16)
            low = jnp.full((1, span), -jnp.inf, F32)
            top = block_max(keys, 0, obs * span, tok, query_out[u], low)
            query_out[u, HEAD_DIM:, :] = offset_rows(top)
            sums[u] = jnp.zeros(sums.shape[1:], F32)

            @pl.loop(0, obs * patches)
            def _(i):
                sums[u] += weighted(keys, values, pl.multiple_of(i * tok, tok), tok, query_out[u])

            send(u).start()
            send(u).wait()


def observed_part(packed, views, obs):
    sources, rows, tok = packed.shape
    span = sources // 2 * tok
    vmem = pl.BlockSpec(memory_space=pltpu.VMEM)
    return pl.pallas_call(
        observed_kernel,
        in_specs=[vmem],
        out_specs=[vmem, pl.BlockSpec(memory_space=pltpu.MemorySpace.HBM)],
        out_shape=[
            jax.ShapeDtypeStruct((views, KEY_COLS, span), BF16),
            pltpu.MemorySpace.HBM((views, VALUE_ROWS, span), F32),
        ],
        scratch_shapes=[
            pltpu.VMEM((obs * span, KEY_COLS), BF16),
            pltpu.VMEM((VALUE_ROWS, obs * span), BF16),
            pltpu.VMEM((views, VALUE_ROWS, span), F32),
            pltpu.SemaphoreType.DMA((views,)),
        ],
        compiler_params=params(32),
        cost_estimate=cost(8 * views * obs * span * span * HEAD_DIM, 4 * MIB),
        name="observed_part",
    )(packed)


def generated_kernel(view_set, view, query, before, packed, out, keys, values, sums, pairs, early, sem):
    patches = packed.shape[0]
    tok = packed.shape[2]
    views = query.shape[0]
    here = views // 2
    span = patches * tok
    fetch = pltpu.make_async_copy(before, early, sem)
    fetch.start()

    def key_set(w):
        return view_set[jnp.bitwise_xor(w, here * view[0])]

    count = jnp.int32(0)
    for u in range(views):
        for w in range(views):
            pairs[count] = u * views + w
            count = count + (view_set[u] == key_set(w)).astype(jnp.int32)
    for w in range(views):
        base = (w // here * 2 * here + w % here) * HEAD_DIM
        for p in range(patches):
            at = (w * patches + p) * tok
            store_keys(keys, at, packed[p, base : base + HEAD_DIM, :])
            value_base = base + here * HEAD_DIM
            values[0:HEAD_DIM, at : at + tok] = packed[p, value_base : value_base + HEAD_DIM, :]
    values[HEAD_DIM:, :] = jnp.ones((VALUE_ROWS - HEAD_DIM, views * span), BF16)
    sums[...] = jnp.zeros(sums.shape, F32)

    def one_pair(i):
        u = pairs[i] // views
        start = pl.multiple_of((pairs[i] % views) * span, span)
        return u, weighted(keys, values, start, span, query[u])

    def several(first, width):
        for u, term in [one_pair(first + i) for i in range(width)]:
            sums[u] += term

    @pl.when(count % 5 == 0)
    def _():
        @pl.loop(0, count // 5)
        def _(i):
            several(5 * i, 5)

    @pl.when(count % 5 != 0)
    def _():
        @pl.loop(0, count // 4)
        def _(i):
            several(4 * i, 4)

    largest = jnp.max(sums[:, SUM_ROW : SUM_ROW + 1, :])
    fetch.wait()

    @pl.when(jnp.logical_not(largest < LIMIT))
    def _():
        @pl.loop(0, views)
        def _(u):
            rows = -query[u, HEAD_DIM : HEAD_DIM + 16, :].astype(F32)
            old = rows[0:1] + rows[1:2] + rows[2:3]
            plain = jnp.concatenate(
                [query[u, 0:HEAD_DIM, :], jnp.zeros((KEY_COLS - HEAD_DIM, span), BF16)], axis=0
            )

            def look(w, top):
                seen = jnp.where(view_set[u] == key_set(w), span, 0)
                return block_max(keys, w * span, seen, tok, plain, top)

            top = lax.fori_loop(0, views, look, old)
            shifted = jnp.concatenate([query[u, 0:HEAD_DIM, :], offset_rows(top)], axis=0)
            early[u] = early[u] * jnp.exp(old - top)
            sums[u] = jnp.zeros(sums.shape[1:], F32)

            @pl.loop(0, views)
            def _(w):
                @pl.when(view_set[u] == key_set(w))
                def _():
                    @pl.loop(0, patches)
                    def _(p):
                        start = pl.multiple_of(w * span + p * tok, tok)
                        sums[u] += weighted(keys, values, start, tok, shifted)

    for u in range(views):
        total = sums[u] + early[u]
        context = (total[0:HEAD_DIM] * (1.0 / total[SUM_ROW : SUM_ROW + 1])).astype(BF16)
        rows = slice((u % here) * HEAD_DIM, (u % here + 1) * HEAD_DIM)
        for p in range(patches):
            out[(u // here) * patches + p, rows, :] = context[:, p * tok : (p + 1) * tok]


def generated_part(view_set, view, query, before, packed):
    patches, rows, tok = packed.shape
    views, _, span = query.shape
    vmem = pl.BlockSpec(memory_space=pltpu.VMEM)
    return pl.pallas_call(
        generated_kernel,
        in_specs=[
            pl.BlockSpec(memory_space=pltpu.SMEM),
            pl.BlockSpec(memory_space=pltpu.SMEM),
            vmem,
            pl.BlockSpec(memory_space=pltpu.MemorySpace.HBM),
            vmem,
        ],
        out_specs=vmem,
        out_shape=jax.ShapeDtypeStruct((2 * patches, rows // 4, tok), BF16),
        scratch_shapes=[
            pltpu.VMEM((views * span, KEY_COLS), BF16),
            pltpu.VMEM((VALUE_ROWS, views * span), BF16),
            pltpu.VMEM((views, VALUE_ROWS, span), F32),
            pltpu.SMEM((views * views + 1,), jnp.int32),
            pltpu.VMEM((views, VALUE_ROWS, span), F32),
            pltpu.SemaphoreType.DMA,
        ],
        compiler_params=params(32),
        cost_estimate=cost(6 * views * views * span * span * HEAD_DIM, 4 * MIB),
        name="generated_part",
    )(view_set, view, query, pltpu.with_memory_space_constraint(before, pltpu.MemorySpace.HBM), packed)


def project_out_kernel(packed, weight, out, context, blocks, sems):
    views, tok = out.shape[:2]
    for i in range(views):
        rows = packed[:, i * HEAD_DIM : (i + 1) * HEAD_DIM, :].reshape(HEADS * HEAD_DIM, tok)
        context[i * tok : (i + 1) * tok, :] = rows.T
    copies = []
    cols = weight.shape[1] // 2
    for j in range(2):
        at = slice(j * cols, (j + 1) * cols)
        blocks[:, :, at] = dot(context[...], weight[:, at]).astype(BF16).reshape(views, tok, cols)
        copies.append(pltpu.make_async_copy(blocks.at[:, :, at], out.at[:, :, at], sems.at[j]))
        copies[j].start()
    for c in copies:
        c.wait()


def project_out(packed, weight):
    heads, rows, tok = packed.shape
    views = rows // HEAD_DIM
    width = weight.shape[0]
    vmem = pl.BlockSpec(memory_space=pltpu.VMEM)
    return pl.pallas_call(
        project_out_kernel,
        in_specs=[vmem, vmem],
        out_specs=pl.BlockSpec(memory_space=pltpu.MemorySpace.HBM),
        out_shape=jax.ShapeDtypeStruct((views, tok, width), BF16),
        scratch_shapes=[
            pltpu.VMEM((views * tok, width), BF16),
            pltpu.VMEM((views, tok, width), BF16),
            pltpu.SemaphoreType.DMA((2,)),
        ],
        compiler_params=params(24),
        cost_estimate=cost(2 * views * tok * width * width, 4 * MIB),
        name="project_out",
    )(packed, weight)


def exchange(blocks):
    return lax.all_to_all(blocks, ("view", "patch"), split_axis=0, concat_axis=0, tiled=True)


def on_device(hidden, rays, view_set, obs_keys, obs_values, w_query, w_key, w_value, w_out):
    views = view_set.shape[0]
    view = lax.axis_index("view").astype(jnp.int32).reshape(1)
    queries = exchange(pack_queries(view, hidden, rays, w_query, obs_keys, obs_values))
    keep, give = pack_pairs(view, hidden, rays, w_key, w_value)
    got = lax.ppermute(give, "view", [(0, 1), (1, 0)])
    pairs = jnp.concatenate([keep, got], axis=1)
    pairs = lax.all_to_all(
        pairs, "patch", split_axis=0, concat_axis=0, tiled=True, axis_index_groups=[list(PATCHES)]
    )
    query, before = observed_part(queries, views, obs_keys.shape[0])
    context = exchange(generated_part(view_set, view, query, before, pairs))
    return project_out(context, w_out)


def solution(mesh):
    return jax.shard_map(
        on_device,
        mesh=mesh,
        in_specs=(
            P(("group", "view"), "patch", None),
            P(("group", "view"), "patch", None),
            P("group"),
            P(None, "patch", None),
            P(None, "patch", None),
            P(),
            P(),
            P(),
            P(),
        ),
        out_specs=P(("group", "view"), "patch", None),
        check_vma=False,
    )
```

```python
import jax
import jax.numpy as jnp
from jax import lax
from jax.experimental import pallas as pl
from jax.experimental.pallas import tpu as pltpu
from jax.sharding import PartitionSpec as P

HEADS = 16
HEAD_DIM = 64
SUM_ROW = HEAD_DIM
VALUE_ROWS = HEAD_DIM + 16
KEY_COLS = 2 * HEAD_DIM
FIRST_KEYS = 32
LIMIT = 2.0**100
BF16 = jnp.bfloat16
F32 = jnp.float32
MIB = 2**20


def dot(a, b):
    return jnp.dot(a, b, preferred_element_type=F32)


def params(mib):
    return pltpu.CompilerParams(vmem_limit_bytes=mib * MIB)


def cost(flops, nbytes):
    return pl.CostEstimate(flops=int(flops), bytes_accessed=int(nbytes), transcendentals=0)


HBM = pl.BlockSpec(memory_space=pltpu.MemorySpace.HBM)
COLUMNS = 2


def column_loads(weight, held, sems, first):
    cols = weight.shape[1] // COLUMNS
    return [
        pltpu.make_async_copy(
            weight.at[:, j * cols : (j + 1) * cols], held.at[:, j * cols : (j + 1) * cols], sems.at[first + j]
        )
        for j in range(COLUMNS)
    ]


def make_source(hid, ray, source):
    both = hid[...].astype(F32) + ray[...].astype(F32)
    source[...] = both.astype(BF16).reshape(source.shape)


def place(blocks, first, base, feats, count, tok):
    for head in range(feats.shape[0] // HEAD_DIM):
        rows = slice(head * HEAD_DIM, (head + 1) * HEAD_DIM)
        for i in range(count):
            at = (base + i) * HEAD_DIM
            blocks[first + head, at : at + HEAD_DIM, :] = feats[rows, i * tok : (i + 1) * tok]


def pack_queries_kernel(
    view, hidden, rays, weight, obs_k, obs_v, out, hid, ray, held, obs, source, blocks, in_sem, out_sem
):
    views, tok = hidden.shape[:2]
    inputs = [pltpu.make_async_copy(hidden, hid, in_sem.at[0]), pltpu.make_async_copy(rays, ray, in_sem.at[1])]
    observed = [pltpu.make_async_copy(o, obs, in_sem.at[2]) for o in (obs_k, obs_v)]
    columns = column_loads(weight, held, in_sem, 3)
    for kind in range(2):

        @pl.when(view[0] == kind)
        def _():
            observed[kind].start()

    for c in inputs + columns:
        c.start()
    base = views * HEAD_DIM
    sends = []

    def send(place_of):
        sends.append(pltpu.make_async_copy(blocks.at[place_of], out.at[place_of], out_sem.at[len(sends)]))
        sends[-1].start()

    observed[0].wait()
    place(blocks, 0, views, obs[...].reshape(-1, obs.shape[-1]).T, obs.shape[0], tok)
    send((slice(None), slice(base, None)))
    for c in inputs:
        c.wait()
    make_source(hid, ray, source)
    cols = weight.shape[1] // COLUMNS
    heads = HEADS // COLUMNS
    for j in range(COLUMNS):
        columns[j].wait()
        feats = dot(source[...], held[:, j * cols : (j + 1) * cols]).astype(BF16) * jnp.asarray(HEAD_DIM**-0.5, BF16)
        place(blocks, j * heads, 0, feats.T, views, tok)
        send((slice(j * heads, (j + 1) * heads), slice(0, base)))
    for c in sends:
        c.wait()


def pack_queries(view, hidden, rays, weight, obs_k, obs_v):
    views, tok, width = hidden.shape
    shape = (HEADS, (views + obs_k.shape[0]) * HEAD_DIM, tok)
    return pl.pallas_call(
        pack_queries_kernel,
        in_specs=[pl.BlockSpec(memory_space=pltpu.SMEM)] + [HBM] * 5,
        out_specs=HBM,
        out_shape=jax.ShapeDtypeStruct(shape, BF16),
        scratch_shapes=[
            pltpu.VMEM(hidden.shape, BF16),
            pltpu.VMEM(rays.shape, BF16),
            pltpu.VMEM(weight.shape, BF16),
            pltpu.VMEM(obs_k.shape, BF16),
            pltpu.VMEM((views * tok, width), BF16),
            pltpu.VMEM(shape, BF16),
            pltpu.SemaphoreType.DMA((3 + COLUMNS,)),
            pltpu.SemaphoreType.DMA((1 + COLUMNS,)),
        ],
        compiler_params=params(58),
        cost_estimate=cost(2 * views * tok * width * width, 6 * MIB),
        name="pack_queries",
    )(view, hidden, rays, weight, obs_k, obs_v)


def pack_pairs_kernel(
    view, hidden, rays, w_key, w_value, keep, give, hid, ray, held_k, held_v, source, blocks, in_sem, out_sem
):
    views, tok = hidden.shape[:2]
    inputs = [pltpu.make_async_copy(hidden, hid, in_sem.at[0]), pltpu.make_async_copy(rays, ray, in_sem.at[1])]
    columns = column_loads(w_key, held_k, in_sem, 2) + column_loads(w_value, held_v, in_sem, 2 + COLUMNS)
    for c in inputs + columns:
        c.start()
    for c in inputs:
        c.wait()
    make_source(hid, ray, source)
    cols = w_key.shape[1] // COLUMNS
    heads = HEADS // COLUMNS
    for i, held in enumerate((held_k, held_v)):
        for j in range(COLUMNS):
            columns[i * COLUMNS + j].wait()
            feats = dot(source[...], held[:, j * cols : (j + 1) * cols]).astype(BF16)
            place(blocks, j * heads, i * views, feats.T, views, tok)
    half = keep.shape[0]
    sends = [
        pltpu.make_async_copy(blocks.at[pl.ds(side * half, half)], out, out_sem.at[i])
        for i, (side, out) in enumerate(((view[0], keep), (1 - view[0], give)))
    ]
    for c in sends:
        c.start()
    for c in sends:
        c.wait()


def pack_pairs(view, hidden, rays, w_key, w_value):
    views, tok, width = hidden.shape
    shape = (HEADS, 2 * views * HEAD_DIM, tok)
    return pl.pallas_call(
        pack_pairs_kernel,
        in_specs=[pl.BlockSpec(memory_space=pltpu.SMEM)] + [HBM] * 4,
        out_specs=[HBM, HBM],
        out_shape=[jax.ShapeDtypeStruct((HEADS // 2,) + shape[1:], BF16)] * 2,
        scratch_shapes=[
            pltpu.VMEM(hidden.shape, BF16),
            pltpu.VMEM(rays.shape, BF16),
            pltpu.VMEM(w_key.shape, BF16),
            pltpu.VMEM(w_value.shape, BF16),
            pltpu.VMEM((views * tok, width), BF16),
            pltpu.VMEM(shape, BF16),
            pltpu.SemaphoreType.DMA((2 + 2 * COLUMNS,)),
            pltpu.SemaphoreType.DMA((2,)),
        ],
        compiler_params=params(58),
        cost_estimate=cost(4 * views * tok * width * width, 7 * MIB),
        name="pack_pairs",
    )(view, hidden, rays, w_key, w_value)


def ones_rows(count, ones, lanes):
    row = lax.broadcasted_iota(jnp.int32, (count, lanes), 0)
    return jnp.where(row < ones, 1.0, 0.0).astype(BF16)


def store_keys(keys, at, turned):
    tok = turned.shape[1]
    full = jnp.concatenate([turned, ones_rows(KEY_COLS - HEAD_DIM, 3, tok)], axis=0)
    keys[at : at + tok, :] = full.T


def offset_rows(top):
    first = top.astype(BF16)
    rest = top - first.astype(F32)
    second = rest.astype(BF16)
    third = rest - second.astype(F32)
    row = lax.broadcasted_iota(jnp.int32, (KEY_COLS - HEAD_DIM, top.shape[1]), 0)
    picked = jnp.where(row == 0, first.astype(F32), 0.0)
    picked = jnp.where(row == 1, second.astype(F32), picked)
    picked = jnp.where(row == 2, third, picked)
    return (-picked).astype(BF16)


def block_max(keys, at, count, block, query, top):
    def step(i, top):
        start = pl.multiple_of(at + i * block, block)
        scores = dot(keys[pl.ds(start, block), :], query)
        return jnp.maximum(top, jnp.max(scores, axis=0, keepdims=True))

    return lax.fori_loop(0, count // block, step, top)


def weighted(keys, values, start, count, query):
    weights = jnp.exp(dot(keys[pl.ds(start, count), :], query)).astype(BF16)
    return dot(values[:, pl.ds(start, count)], weights)


def observed_kernel(packed, query_out, sums_out, keys, values, sums, sems):
    patches = packed.shape[0] // 2
    tok = packed.shape[2]
    views = query_out.shape[0]
    here = views // 2
    obs = packed.shape[1] // HEAD_DIM - here
    span = patches * tok
    for o in range(obs):
        rows = slice((here + o) * HEAD_DIM, (here + o + 1) * HEAD_DIM)
        for p in range(patches):
            at = (o * patches + p) * tok
            store_keys(keys, at, packed[p, rows, :])
            values[0:HEAD_DIM, at : at + tok] = packed[patches + p, rows, :]
    values[HEAD_DIM:, :] = jnp.ones((VALUE_ROWS - HEAD_DIM, obs * span), BF16)
    for u in range(views):
        rows = slice((u % here) * HEAD_DIM, (u % here + 1) * HEAD_DIM)
        query = jnp.concatenate([packed[(u // here) * patches + p, rows, :] for p in range(patches)], axis=1)
        query_out[u, 0:HEAD_DIM, :] = query
        top = jnp.max(dot(keys[0:FIRST_KEYS, 0:HEAD_DIM], query), axis=0, keepdims=True)
        query_out[u, HEAD_DIM:, :] = offset_rows(top)

    def one_view(u, block):
        query = query_out[u]
        total = None
        for o in range(obs * span // block):
            term = weighted(keys, values, o * block, block, query)
            total = term if total is None else total + term
        sums[u] = total

    def send(u):
        return pltpu.make_async_copy(sums.at[u], sums_out.at[u], sems.at[u])

    @pl.loop(0, views // 2)
    def _(i):
        for u in (2 * i, 2 * i + 1):
            one_view(u, span)
            send(u).start()

    largest = jnp.max(sums[:, SUM_ROW : SUM_ROW + 1, :])
    for u in range(views):
        send(u).wait()

    @pl.when(jnp.logical_not(largest < LIMIT))
    def _():
        @pl.loop(0, views)
        def _(u):
            query_out[u, HEAD_DIM:, :] = jnp.zeros((KEY_COLS - HEAD_DIM, span), BF16)
            low = jnp.full((1, span), -jnp.inf, F32)
            top = block_max(keys, 0, obs * span, tok, query_out[u], low)
            query_out[u, HEAD_DIM:, :] = offset_rows(top)
            sums[u] = jnp.zeros(sums.shape[1:], F32)

            @pl.loop(0, obs * patches)
            def _(i):
                sums[u] += weighted(keys, values, pl.multiple_of(i * tok, tok), tok, query_out[u])

            send(u).start()
            send(u).wait()


def observed_part(packed, views, obs):
    sources, rows, tok = packed.shape
    span = sources // 2 * tok
    vmem = pl.BlockSpec(memory_space=pltpu.VMEM)
    return pl.pallas_call(
        observed_kernel,
        in_specs=[vmem],
        out_specs=[vmem, pl.BlockSpec(memory_space=pltpu.MemorySpace.HBM)],
        out_shape=[
            jax.ShapeDtypeStruct((views, KEY_COLS, span), BF16),
            pltpu.MemorySpace.HBM((views, VALUE_ROWS, span), F32),
        ],
        scratch_shapes=[
            pltpu.VMEM((obs * span, KEY_COLS), BF16),
            pltpu.VMEM((VALUE_ROWS, obs * span), BF16),
            pltpu.VMEM((views, VALUE_ROWS, span), F32),
            pltpu.SemaphoreType.DMA((views,)),
        ],
        compiler_params=params(32),
        cost_estimate=cost(8 * views * obs * span * span * HEAD_DIM, 4 * MIB),
        name="observed_part",
    )(packed)


def generated_kernel(view_set, view, query, before, packed, out, keys, values, sums, pairs, early, sem):
    patches = packed.shape[0]
    tok = packed.shape[2]
    views = query.shape[0]
    here = views // 2
    span = patches * tok
    fetch = pltpu.make_async_copy(before, early, sem)
    fetch.start()

    def key_set(w):
        return view_set[jnp.bitwise_xor(w, here * view[0])]

    count = jnp.int32(0)
    for u in range(views):
        for w in range(views):
            pairs[count] = u * views + w
            count = count + (view_set[u] == key_set(w)).astype(jnp.int32)
    for w in range(views):
        base = (w // here * 2 * here + w % here) * HEAD_DIM
        for p in range(patches):
            at = (w * patches + p) * tok
            store_keys(keys, at, packed[p, base : base + HEAD_DIM, :])
            value_base = base + here * HEAD_DIM
            values[0:HEAD_DIM, at : at + tok] = packed[p, value_base : value_base + HEAD_DIM, :]
    values[HEAD_DIM:, :] = jnp.ones((VALUE_ROWS - HEAD_DIM, views * span), BF16)
    sums[...] = jnp.zeros(sums.shape, F32)

    def one_pair(i):
        u = pairs[i] // views
        start = pl.multiple_of((pairs[i] % views) * span, span)
        return u, weighted(keys, values, start, span, query[u])

    def several(first, width):
        for u, term in [one_pair(first + i) for i in range(width)]:
            sums[u] += term

    @pl.when(count % 5 == 0)
    def _():
        @pl.loop(0, count // 5)
        def _(i):
            several(5 * i, 5)

    @pl.when(count % 5 != 0)
    def _():
        @pl.loop(0, count // 4)
        def _(i):
            several(4 * i, 4)

    largest = jnp.max(sums[:, SUM_ROW : SUM_ROW + 1, :])
    fetch.wait()

    @pl.when(jnp.logical_not(largest < LIMIT))
    def _():
        @pl.loop(0, views)
        def _(u):
            rows = -query[u, HEAD_DIM : HEAD_DIM + 16, :].astype(F32)
            old = rows[0:1] + rows[1:2] + rows[2:3]
            plain = jnp.concatenate(
                [query[u, 0:HEAD_DIM, :], jnp.zeros((KEY_COLS - HEAD_DIM, span), BF16)], axis=0
            )

            def look(w, top):
                seen = jnp.where(view_set[u] == key_set(w), span, 0)
                return block_max(keys, w * span, seen, tok, plain, top)

            top = lax.fori_loop(0, views, look, old)
            shifted = jnp.concatenate([query[u, 0:HEAD_DIM, :], offset_rows(top)], axis=0)
            early[u] = early[u] * jnp.exp(old - top)
            sums[u] = jnp.zeros(sums.shape[1:], F32)

            @pl.loop(0, views)
            def _(w):
                @pl.when(view_set[u] == key_set(w))
                def _():
                    @pl.loop(0, patches)
                    def _(p):
                        start = pl.multiple_of(w * span + p * tok, tok)
                        sums[u] += weighted(keys, values, start, tok, shifted)

    for u in range(views):
        total = sums[u] + early[u]
        context = (total[0:HEAD_DIM] * (1.0 / total[SUM_ROW : SUM_ROW + 1])).astype(BF16)
        rows = slice((u % here) * HEAD_DIM, (u % here + 1) * HEAD_DIM)
        for p in range(patches):
            out[(u // here) * patches + p, rows, :] = context[:, p * tok : (p + 1) * tok]


def generated_part(view_set, view, query, before, packed):
    patches, rows, tok = packed.shape
    views, _, span = query.shape
    vmem = pl.BlockSpec(memory_space=pltpu.VMEM)
    return pl.pallas_call(
        generated_kernel,
        in_specs=[
            pl.BlockSpec(memory_space=pltpu.SMEM),
            pl.BlockSpec(memory_space=pltpu.SMEM),
            vmem,
            pl.BlockSpec(memory_space=pltpu.MemorySpace.HBM),
            vmem,
        ],
        out_specs=vmem,
        out_shape=jax.ShapeDtypeStruct((2 * patches, rows // 4, tok), BF16),
        scratch_shapes=[
            pltpu.VMEM((views * span, KEY_COLS), BF16),
            pltpu.VMEM((VALUE_ROWS, views * span), BF16),
            pltpu.VMEM((views, VALUE_ROWS, span), F32),
            pltpu.SMEM((views * views + 1,), jnp.int32),
            pltpu.VMEM((views, VALUE_ROWS, span), F32),
            pltpu.SemaphoreType.DMA,
        ],
        compiler_params=params(32),
        cost_estimate=cost(6 * views * views * span * span * HEAD_DIM, 4 * MIB),
        name="generated_part",
    )(view_set, view, query, pltpu.with_memory_space_constraint(before, pltpu.MemorySpace.HBM), packed)


def project_out_kernel(packed, weight, out, context, blocks, sems):
    views, tok = out.shape[:2]
    for i in range(views):
        rows = packed[:, i * HEAD_DIM : (i + 1) * HEAD_DIM, :].reshape(HEADS * HEAD_DIM, tok)
        context[i * tok : (i + 1) * tok, :] = rows.T
    copies = []
    parts = sems.shape[0]
    cols = weight.shape[1] // parts
    for j in range(parts):
        at = slice(j * cols, (j + 1) * cols)
        blocks[:, :, at] = dot(context[...], weight[:, at]).astype(BF16).reshape(views, tok, cols)
        copies.append(pltpu.make_async_copy(blocks.at[:, :, at], out.at[:, :, at], sems.at[j]))
        copies[j].start()
    for c in copies:
        c.wait()


def project_out(packed, weight):
    heads, rows, tok = packed.shape
    views = rows // HEAD_DIM
    width = weight.shape[0]
    vmem = pl.BlockSpec(memory_space=pltpu.VMEM)
    return pl.pallas_call(
        project_out_kernel,
        in_specs=[vmem, vmem],
        out_specs=pl.BlockSpec(memory_space=pltpu.MemorySpace.HBM),
        out_shape=jax.ShapeDtypeStruct((views, tok, width), BF16),
        scratch_shapes=[
            pltpu.VMEM((views * tok, width), BF16),
            pltpu.VMEM((views, tok, width), BF16),
            pltpu.SemaphoreType.DMA((4,)),
        ],
        compiler_params=params(24),
        cost_estimate=cost(2 * views * tok * width * width, 4 * MIB),
        name="project_out",
    )(packed, weight)


def exchange(blocks):
    return lax.all_to_all(blocks, ("view", "patch"), split_axis=0, concat_axis=0, tiled=True)


def on_device(hidden, rays, view_set, obs_keys, obs_values, w_query, w_key, w_value, w_out):
    views = view_set.shape[0]
    view = lax.axis_index("view").astype(jnp.int32).reshape(1)
    queries = exchange(pack_queries(view, hidden, rays, w_query, obs_keys, obs_values))
    keep, give = pack_pairs(view, hidden, rays, w_key, w_value)
    got = lax.ppermute(give, "view", [(0, 1), (1, 0)])
    pairs = jnp.concatenate([keep, got], axis=1)
    pairs = lax.all_to_all(pairs, "patch", split_axis=0, concat_axis=0, tiled=True)
    query, before = observed_part(queries, views, obs_keys.shape[0])
    context = exchange(generated_part(view_set, view, query, before, pairs))
    return project_out(context, w_out)


def solution(mesh):
    return jax.shard_map(
        on_device,
        mesh=mesh,
        in_specs=(
            P(("group", "view"), "patch", None),
            P(("group", "view"), "patch", None),
            P("group"),
            P(None, "patch", None),
            P(None, "patch", None),
            P(),
            P(),
            P(),
            P(),
        ),
        out_specs=P(("group", "view"), "patch", None),
        check_vma=False,
    )
```

```python
import jax
import jax.numpy as jnp
from jax import lax
from jax.experimental import pallas as pl
from jax.experimental.pallas import tpu as pltpu
from jax.sharding import PartitionSpec as P

HEADS = 16
HEAD_DIM = 64
SUM_ROW = HEAD_DIM
VALUE_ROWS = HEAD_DIM + 16
KEY_COLS = 2 * HEAD_DIM
FIRST_KEYS = 32
LIMIT = 2.0**100
BF16 = jnp.bfloat16
F32 = jnp.float32
MIB = 2**20


def dot(a, b):
    return jnp.dot(a, b, preferred_element_type=F32)


def params(mib):
    return pltpu.CompilerParams(vmem_limit_bytes=mib * MIB)


def cost(flops, nbytes):
    return pl.CostEstimate(flops=int(flops), bytes_accessed=int(nbytes), transcendentals=0)


HBM = pl.BlockSpec(memory_space=pltpu.MemorySpace.HBM)
COLUMNS = 2


def column_loads(weight, held, sems, first):
    cols = weight.shape[1] // COLUMNS
    return [
        pltpu.make_async_copy(
            weight.at[:, j * cols : (j + 1) * cols], held.at[:, j * cols : (j + 1) * cols], sems.at[first + j]
        )
        for j in range(COLUMNS)
    ]


def make_source(hid, ray, source):
    both = hid[...].astype(F32) + ray[...].astype(F32)
    source[...] = both.astype(BF16).reshape(source.shape)


def place(blocks, first, base, feats, count, tok):
    for head in range(feats.shape[0] // HEAD_DIM):
        rows = slice(head * HEAD_DIM, (head + 1) * HEAD_DIM)
        for i in range(count):
            at = (base + i) * HEAD_DIM
            blocks[first + head, at : at + HEAD_DIM, :] = feats[rows, i * tok : (i + 1) * tok]


def pack_queries_kernel(
    view, hidden, rays, weight, obs_k, obs_v, out, hid, ray, held, obs, source, blocks, in_sem, out_sem
):
    views, tok = hidden.shape[:2]
    inputs = [pltpu.make_async_copy(hidden, hid, in_sem.at[0]), pltpu.make_async_copy(rays, ray, in_sem.at[1])]
    observed = [pltpu.make_async_copy(o, obs, in_sem.at[2]) for o in (obs_k, obs_v)]
    columns = column_loads(weight, held, in_sem, 3)
    for kind in range(2):

        @pl.when(view[0] == kind)
        def _():
            observed[kind].start()

    for c in inputs + columns:
        c.start()
    base = views * HEAD_DIM
    sends = []

    def send(place_of):
        sends.append(pltpu.make_async_copy(blocks.at[place_of], out.at[place_of], out_sem.at[len(sends)]))
        sends[-1].start()

    observed[0].wait()
    place(blocks, 0, views, obs[...].reshape(-1, obs.shape[-1]).T, obs.shape[0], tok)
    send((slice(None), slice(base, None)))
    for c in inputs:
        c.wait()
    make_source(hid, ray, source)
    cols = weight.shape[1] // COLUMNS
    heads = HEADS // COLUMNS
    for j in range(COLUMNS):
        columns[j].wait()
        feats = dot(source[...], held[:, j * cols : (j + 1) * cols]).astype(BF16) * jnp.asarray(HEAD_DIM**-0.5, BF16)
        place(blocks, j * heads, 0, feats.T, views, tok)
        send((slice(j * heads, (j + 1) * heads), slice(0, base)))
    for c in sends:
        c.wait()


def pack_queries(view, hidden, rays, weight, obs_k, obs_v):
    views, tok, width = hidden.shape
    shape = (HEADS, (views + obs_k.shape[0]) * HEAD_DIM, tok)
    return pl.pallas_call(
        pack_queries_kernel,
        in_specs=[pl.BlockSpec(memory_space=pltpu.SMEM)] + [HBM] * 5,
        out_specs=HBM,
        out_shape=jax.ShapeDtypeStruct(shape, BF16),
        scratch_shapes=[
            pltpu.VMEM(hidden.shape, BF16),
            pltpu.VMEM(rays.shape, BF16),
            pltpu.VMEM(weight.shape, BF16),
            pltpu.VMEM(obs_k.shape, BF16),
            pltpu.VMEM((views * tok, width), BF16),
            pltpu.VMEM(shape, BF16),
            pltpu.SemaphoreType.DMA((3 + COLUMNS,)),
            pltpu.SemaphoreType.DMA((1 + COLUMNS,)),
        ],
        compiler_params=params(58),
        cost_estimate=cost(2 * views * tok * width * width, 6 * MIB),
        name="pack_queries",
    )(view, hidden, rays, weight, obs_k, obs_v)


def pack_pairs_kernel(
    view, hidden, rays, w_key, w_value, keep, give, hid, ray, held_k, held_v, source, blocks, in_sem, out_sem
):
    views, tok = hidden.shape[:2]
    inputs = [pltpu.make_async_copy(hidden, hid, in_sem.at[0]), pltpu.make_async_copy(rays, ray, in_sem.at[1])]
    columns = column_loads(w_key, held_k, in_sem, 2) + column_loads(w_value, held_v, in_sem, 2 + COLUMNS)
    for c in inputs + columns:
        c.start()
    for c in inputs:
        c.wait()
    make_source(hid, ray, source)
    cols = w_key.shape[1] // COLUMNS
    heads = HEADS // COLUMNS
    for i, held in enumerate((held_k, held_v)):
        for j in range(COLUMNS):
            columns[i * COLUMNS + j].wait()
            feats = dot(source[...], held[:, j * cols : (j + 1) * cols]).astype(BF16)
            place(blocks, j * heads, i * views, feats.T, views, tok)
    half = keep.shape[0]
    sends = [
        pltpu.make_async_copy(blocks.at[pl.ds(side * half, half)], out, out_sem.at[i])
        for i, (side, out) in enumerate(((view[0], keep), (1 - view[0], give)))
    ]
    for c in sends:
        c.start()
    for c in sends:
        c.wait()


def pack_pairs(view, hidden, rays, w_key, w_value):
    views, tok, width = hidden.shape
    shape = (HEADS, 2 * views * HEAD_DIM, tok)
    return pl.pallas_call(
        pack_pairs_kernel,
        in_specs=[pl.BlockSpec(memory_space=pltpu.SMEM)] + [HBM] * 4,
        out_specs=[HBM, HBM],
        out_shape=[jax.ShapeDtypeStruct((HEADS // 2,) + shape[1:], BF16)] * 2,
        scratch_shapes=[
            pltpu.VMEM(hidden.shape, BF16),
            pltpu.VMEM(rays.shape, BF16),
            pltpu.VMEM(w_key.shape, BF16),
            pltpu.VMEM(w_value.shape, BF16),
            pltpu.VMEM((views * tok, width), BF16),
            pltpu.VMEM(shape, BF16),
            pltpu.SemaphoreType.DMA((2 + 2 * COLUMNS,)),
            pltpu.SemaphoreType.DMA((2,)),
        ],
        compiler_params=params(58),
        cost_estimate=cost(4 * views * tok * width * width, 7 * MIB),
        name="pack_pairs",
    )(view, hidden, rays, w_key, w_value)


def ones_rows(count, ones, lanes):
    row = lax.broadcasted_iota(jnp.int32, (count, lanes), 0)
    return jnp.where(row < ones, 1.0, 0.0).astype(BF16)


def store_keys(keys, at, turned):
    tok = turned.shape[1]
    full = jnp.concatenate([turned, ones_rows(KEY_COLS - HEAD_DIM, 3, tok)], axis=0)
    keys[at : at + tok, :] = full.T


def offset_rows(top):
    first = top.astype(BF16)
    rest = top - first.astype(F32)
    second = rest.astype(BF16)
    third = rest - second.astype(F32)
    row = lax.broadcasted_iota(jnp.int32, (KEY_COLS - HEAD_DIM, top.shape[1]), 0)
    picked = jnp.where(row == 0, first.astype(F32), 0.0)
    picked = jnp.where(row == 1, second.astype(F32), picked)
    picked = jnp.where(row == 2, third, picked)
    return (-picked).astype(BF16)


def block_max(keys, at, count, block, query, top):
    def step(i, top):
        start = pl.multiple_of(at + i * block, block)
        scores = dot(keys[pl.ds(start, block), :], query)
        return jnp.maximum(top, jnp.max(scores, axis=0, keepdims=True))

    return lax.fori_loop(0, count // block, step, top)


def weighted(keys, values, start, count, query):
    weights = jnp.exp(dot(keys[pl.ds(start, count), :], query)).astype(BF16)
    return dot(values[:, pl.ds(start, count)], weights)


def observed_kernel(packed, query_out, sums_out, keys, values, sums, sems):
    patches = packed.shape[0] // 2
    tok = packed.shape[2]
    views = query_out.shape[0]
    here = views // 2
    obs = packed.shape[1] // HEAD_DIM - here
    span = patches * tok
    for o in range(obs):
        rows = slice((here + o) * HEAD_DIM, (here + o + 1) * HEAD_DIM)
        for p in range(patches):
            at = (o * patches + p) * tok
            store_keys(keys, at, packed[p, rows, :])
            values[0:HEAD_DIM, at : at + tok] = packed[patches + p, rows, :]
    values[HEAD_DIM:, :] = jnp.ones((VALUE_ROWS - HEAD_DIM, obs * span), BF16)
    for u in range(views):
        rows = slice((u % here) * HEAD_DIM, (u % here + 1) * HEAD_DIM)
        query = jnp.concatenate([packed[(u // here) * patches + p, rows, :] for p in range(patches)], axis=1)
        query_out[u, 0:HEAD_DIM, :] = query
        top = jnp.max(dot(keys[0:FIRST_KEYS, 0:HEAD_DIM], query), axis=0, keepdims=True)
        query_out[u, HEAD_DIM:, :] = offset_rows(top)

    def one_view(u, block):
        query = query_out[u]
        total = None
        for o in range(obs * span // block):
            term = weighted(keys, values, o * block, block, query)
            total = term if total is None else total + term
        sums[u] = total

    def send(u):
        return pltpu.make_async_copy(sums.at[u], sums_out.at[u], sems.at[u])

    @pl.loop(0, views)
    def _(u):
        one_view(u, span)
        send(u).start()

    largest = jnp.max(sums[:, SUM_ROW : SUM_ROW + 1, :])
    for u in range(views):
        send(u).wait()

    @pl.when(jnp.logical_not(largest < LIMIT))
    def _():
        @pl.loop(0, views)
        def _(u):
            query_out[u, HEAD_DIM:, :] = jnp.zeros((KEY_COLS - HEAD_DIM, span), BF16)
            low = jnp.full((1, span), -jnp.inf, F32)
            top = block_max(keys, 0, obs * span, tok, query_out[u], low)
            query_out[u, HEAD_DIM:, :] = offset_rows(top)
            sums[u] = jnp.zeros(sums.shape[1:], F32)

            @pl.loop(0, obs * patches)
            def _(i):
                sums[u] += weighted(keys, values, pl.multiple_of(i * tok, tok), tok, query_out[u])

            send(u).start()
            send(u).wait()


def observed_part(packed, views, obs):
    sources, rows, tok = packed.shape
    span = sources // 2 * tok
    vmem = pl.BlockSpec(memory_space=pltpu.VMEM)
    return pl.pallas_call(
        observed_kernel,
        in_specs=[vmem],
        out_specs=[vmem, pl.BlockSpec(memory_space=pltpu.MemorySpace.HBM)],
        out_shape=[
            jax.ShapeDtypeStruct((views, KEY_COLS, span), BF16),
            pltpu.MemorySpace.HBM((views, VALUE_ROWS, span), F32),
        ],
        scratch_shapes=[
            pltpu.VMEM((obs * span, KEY_COLS), BF16),
            pltpu.VMEM((VALUE_ROWS, obs * span), BF16),
            pltpu.VMEM((views, VALUE_ROWS, span), F32),
            pltpu.SemaphoreType.DMA((views,)),
        ],
        compiler_params=params(32),
        cost_estimate=cost(8 * views * obs * span * span * HEAD_DIM, 4 * MIB),
        name="observed_part",
    )(packed)


def generated_kernel(view_set, view, query, before, packed, out, keys, values, sums, pairs, early, sem):
    patches = packed.shape[0]
    tok = packed.shape[2]
    views = query.shape[0]
    here = views // 2
    span = patches * tok
    fetch = pltpu.make_async_copy(before, early, sem)
    fetch.start()

    def key_set(w):
        return view_set[jnp.bitwise_xor(w, here * view[0])]

    count = jnp.int32(0)
    for u in range(views):
        for w in range(views):
            pairs[count] = u * views + w
            count = count + (view_set[u] == key_set(w)).astype(jnp.int32)
    for w in range(views):
        base = (w // here * 2 * here + w % here) * HEAD_DIM
        for p in range(patches):
            at = (w * patches + p) * tok
            store_keys(keys, at, packed[p, base : base + HEAD_DIM, :])
            value_base = base + here * HEAD_DIM
            values[0:HEAD_DIM, at : at + tok] = packed[p, value_base : value_base + HEAD_DIM, :]
    values[HEAD_DIM:, :] = jnp.ones((VALUE_ROWS - HEAD_DIM, views * span), BF16)
    sums[...] = jnp.zeros(sums.shape, F32)

    def one_pair(i):
        u = pairs[i] // views
        start = pl.multiple_of((pairs[i] % views) * span, span)
        return u, weighted(keys, values, start, span, query[u])

    @pl.loop(0, count // 2)
    def _(i):
        u0, term0 = one_pair(2 * i)
        u1, term1 = one_pair(2 * i + 1)
        sums[u0] += term0
        sums[u1] += term1

    largest = jnp.max(sums[:, SUM_ROW : SUM_ROW + 1, :])
    fetch.wait()

    @pl.when(jnp.logical_not(largest < LIMIT))
    def _():
        @pl.loop(0, views)
        def _(u):
            rows = -query[u, HEAD_DIM : HEAD_DIM + 16, :].astype(F32)
            old = rows[0:1] + rows[1:2] + rows[2:3]
            plain = jnp.concatenate(
                [query[u, 0:HEAD_DIM, :], jnp.zeros((KEY_COLS - HEAD_DIM, span), BF16)], axis=0
            )

            def look(w, top):
                seen = jnp.where(view_set[u] == key_set(w), span, 0)
                return block_max(keys, w * span, seen, tok, plain, top)

            top = lax.fori_loop(0, views, look, old)
            shifted = jnp.concatenate([query[u, 0:HEAD_DIM, :], offset_rows(top)], axis=0)
            early[u] = early[u] * jnp.exp(old - top)
            sums[u] = jnp.zeros(sums.shape[1:], F32)

            @pl.loop(0, views)
            def _(w):
                @pl.when(view_set[u] == key_set(w))
                def _():
                    @pl.loop(0, patches)
                    def _(p):
                        start = pl.multiple_of(w * span + p * tok, tok)
                        sums[u] += weighted(keys, values, start, tok, shifted)

    for u in range(views):
        total = sums[u] + early[u]
        context = (total[0:HEAD_DIM] * (1.0 / total[SUM_ROW : SUM_ROW + 1])).astype(BF16)
        rows = slice((u % here) * HEAD_DIM, (u % here + 1) * HEAD_DIM)
        for p in range(patches):
            out[(u // here) * patches + p, rows, :] = context[:, p * tok : (p + 1) * tok]


def generated_part(view_set, view, query, before, packed):
    patches, rows, tok = packed.shape
    views, _, span = query.shape
    vmem = pl.BlockSpec(memory_space=pltpu.VMEM)
    return pl.pallas_call(
        generated_kernel,
        in_specs=[
            pl.BlockSpec(memory_space=pltpu.SMEM),
            pl.BlockSpec(memory_space=pltpu.SMEM),
            vmem,
            pl.BlockSpec(memory_space=pltpu.MemorySpace.HBM),
            vmem,
        ],
        out_specs=vmem,
        out_shape=jax.ShapeDtypeStruct((2 * patches, rows // 4, tok), BF16),
        scratch_shapes=[
            pltpu.VMEM((views * span, KEY_COLS), BF16),
            pltpu.VMEM((VALUE_ROWS, views * span), BF16),
            pltpu.VMEM((views, VALUE_ROWS, span), F32),
            pltpu.SMEM((views * views + 1,), jnp.int32),
            pltpu.VMEM((views, VALUE_ROWS, span), F32),
            pltpu.SemaphoreType.DMA,
        ],
        compiler_params=params(32),
        cost_estimate=cost(6 * views * views * span * span * HEAD_DIM, 4 * MIB),
        name="generated_part",
    )(view_set, view, query, pltpu.with_memory_space_constraint(before, pltpu.MemorySpace.HBM), packed)


def project_out_kernel(packed, weight, out, context, blocks, sems):
    views, tok = out.shape[:2]
    for i in range(views):
        rows = packed[:, i * HEAD_DIM : (i + 1) * HEAD_DIM, :].reshape(HEADS * HEAD_DIM, tok)
        context[i * tok : (i + 1) * tok, :] = rows.T
    copies = []
    cols = weight.shape[1] // 2
    for j in range(2):
        at = slice(j * cols, (j + 1) * cols)
        blocks[:, :, at] = dot(context[...], weight[:, at]).astype(BF16).reshape(views, tok, cols)
        copies.append(pltpu.make_async_copy(blocks.at[:, :, at], out.at[:, :, at], sems.at[j]))
        copies[j].start()
    for c in copies:
        c.wait()


def project_out(packed, weight):
    heads, rows, tok = packed.shape
    views = rows // HEAD_DIM
    width = weight.shape[0]
    vmem = pl.BlockSpec(memory_space=pltpu.VMEM)
    return pl.pallas_call(
        project_out_kernel,
        in_specs=[vmem, vmem],
        out_specs=pl.BlockSpec(memory_space=pltpu.MemorySpace.HBM),
        out_shape=jax.ShapeDtypeStruct((views, tok, width), BF16),
        scratch_shapes=[
            pltpu.VMEM((views * tok, width), BF16),
            pltpu.VMEM((views, tok, width), BF16),
            pltpu.SemaphoreType.DMA((2,)),
        ],
        compiler_params=params(24),
        cost_estimate=cost(2 * views * tok * width * width, 4 * MIB),
        name="project_out",
    )(packed, weight)


def exchange(blocks):
    return lax.all_to_all(blocks, ("view", "patch"), split_axis=0, concat_axis=0, tiled=True)


def on_device(hidden, rays, view_set, obs_keys, obs_values, w_query, w_key, w_value, w_out):
    views = view_set.shape[0]
    view = lax.axis_index("view").astype(jnp.int32).reshape(1)
    queries = exchange(pack_queries(view, hidden, rays, w_query, obs_keys, obs_values))
    keep, give = pack_pairs(view, hidden, rays, w_key, w_value)
    got = lax.ppermute(give, "view", [(0, 1), (1, 0)])
    pairs = jnp.concatenate([keep, got], axis=1)
    pairs = lax.all_to_all(pairs, "patch", split_axis=0, concat_axis=0, tiled=True)
    query, before = observed_part(queries, views, obs_keys.shape[0])
    context = exchange(generated_part(view_set, view, query, before, pairs))
    return project_out(context, w_out)


def solution(mesh):
    return jax.shard_map(
        on_device,
        mesh=mesh,
        in_specs=(
            P(("group", "view"), "patch", None),
            P(("group", "view"), "patch", None),
            P("group"),
            P(None, "patch", None),
            P(None, "patch", None),
            P(),
            P(),
            P(),
            P(),
        ),
        out_specs=P(("group", "view"), "patch", None),
        check_vma=False,
    )
```
